256 devices in a mesh: jobs: 16 (over z, core), tm: 16 (over x, y).
Axes of the slice: x: 4, y: 4, z: 8, core: 2. Of those that a mesh axis runs over, the one named last changes fastest.
Arguments:
- start_density: float32 [16384, 4096], P('jobs', 'tm'), may hold values from 0 to 4
- assign_dual: float32 [16384], P('jobs'), may hold values from -40 to 40
- cap_dual: float32 [2048, 4096], P(None, 'tm'), may hold values from 0 to 2
- tool_of_job: int32 [16384], P('jobs'), may hold values from 0 to 2047
- durations: int32 [16384], P('jobs'), may hold values from 1 to 32, as said below
- releases: int32 [16384], P('jobs'), may hold values from 0 to 4063
- slack: int32 [16384], P('jobs'), may hold values from 0 to 127
- capacity: int32 [2048, 4096], P(None, 'tm'), may hold values from 1 to 7
- job_weight: float32 [16384], P('jobs'), may hold values from 0.5 to 4
- eta: float32 [1], replicated, may hold values from 0.1 to 0.3
- omega: float32 [1], replicated, may hold values from 0.4 to 0.8
Outputs:
- start_out: float32 [16384, 4096], P('jobs', 'tm')
- assign_out: float32 [16384], P('jobs')
- cap_out: float32 [2048, 4096], P('jobs', 'tm')
The draws below stay inside these ranges and needn't reach their ends.
Inputs may be any that keep to these rules, and one draw needn't show every extreme that they name: `durations`: every job occupies 1 to 32 slots, and some job occupies exactly 32.
All inputs are finite; a program needn't handle non-finite values.
Results may differ from the reference program's by a relative error of at most 0.00011.
Values sent between devices are 32-bit elements; how exact they have to be, the bound alone decides.
A program may use at most 64 MiB of HBM per device.

```python
import math
import jax
import jax.numpy as jnp
from jax import lax

K = 2048
WIN = 32
NJOBS = 16384
NT = 4096


def draw_durations(key, part):
    values = jax.random.randint(key, (NJOBS,), 1, WIN + 1)
    return values.at[0].set(WIN).astype(jnp.int32)


def place_ends(entries, own_key, low, high):
    index_at = [jax.random.randint(jax.random.fold_in(own_key, axis), (), 0, length) for axis, length in enumerate(entries.shape)]
    widest = entries.shape.index(max(entries.shape))
    next_to = index_at[:widest] + [(index_at[widest] + 1) % entries.shape[widest]] + index_at[widest + 1:]
    return entries.at[tuple(index_at)].set(low).at[tuple(next_to)].set(high)


def steps_of(stream_key, extent, shards, least, largest):
    loudness, own = 1.0, jax.random.fold_in(stream_key, 6)
    for dim, blocks in shards:
        heights = jnp.exp(jax.random.uniform(jax.random.fold_in(own, dim), (blocks,), jnp.float32, least / len(shards), largest / len(shards)))
        loudness = loudness * jnp.repeat(heights, extent[dim] // blocks).reshape([-1 if axis == dim else 1 for axis in range(len(extent))])
    return loudness


def gaussian(rng, shape, spread, reach, split=(), kind=jnp.bfloat16):
    array = jax.random.normal(rng, shape, jnp.float32) * spread
    if len(split) > 0:
        array = steps_of(rng, shape, split, -0.22, 0.18) * array
    return jnp.clip(array, min=-reach, max=reach).astype(kind)


def setup_inputs(seed: int = 0) -> dict:
    key_list = jax.random.split(jax.random.key(seed), 12)
    start_density = jnp.clip(4.0 * jax.random.uniform(key_list[0], (NJOBS, NT), jnp.float32) ** steps_of(key_list[0], (NJOBS, NT), ((0, 16), (1, 16)), -0.2, 0.2), 0.0, 4.0)
    assign_dual = gaussian(key_list[1], (NJOBS,), 8.0, 40.0, ((0, 16),), jnp.float32)
    cap_dual = jnp.clip(2.0 * jax.random.uniform(key_list[2], (K, NT), jnp.float32) ** steps_of(key_list[2], (K, NT), ((1, 16),), -0.2, 0.2), 0.0, 2.0)
    tool_of_job = place_ends(jax.random.randint(key_list[3], (NJOBS,), 0, K), jax.random.fold_in(key_list[3], 1), 0, K - 1).astype(jnp.int32)
    durations = draw_durations(jax.random.fold_in(key_list[11], 71), 0)
    releases = place_ends(jax.random.randint(key_list[5], (NJOBS,), 0, NT - WIN), jax.random.fold_in(key_list[5], 1), 0, (NT - WIN) - 1).astype(jnp.int32)
    slack = place_ends(jax.random.randint(key_list[6], (NJOBS,), 0, 4 * WIN), jax.random.fold_in(key_list[6], 1), 0, (4 * WIN) - 1).astype(jnp.int32)
    capacity = place_ends(jax.random.randint(key_list[7], (K, NT), 1, 8), jax.random.fold_in(key_list[7], 1), 1, 7).astype(jnp.int32)
    job_weight = jnp.clip(jnp.exp(math.log(4.0) - 2.0794415 * jax.random.uniform(key_list[8], (NJOBS,), jnp.float32) ** steps_of(key_list[8], (NJOBS,), ((0, 16),), -0.2, 0.2)), 0.5, 4.0)
    eta = jnp.clip(jnp.exp(jax.random.uniform(key_list[9], (1,), jnp.float32, math.log(0.1), math.log(0.3))), 0.1, 0.3)
    omega = jnp.clip(jnp.exp(jax.random.uniform(key_list[10], (1,), jnp.float32, math.log(0.4), math.log(0.8))), 0.4, 0.8)
    return {"start_density": start_density, "assign_dual": assign_dual, "cap_dual": cap_dual, "tool_of_job": tool_of_job, "durations": durations, "releases": releases, "slack": slack, "capacity": capacity, "job_weight": job_weight, "eta": eta, "omega": omega}


def window_loads(starts, tool_of_job, durations):
    slots = jnp.arange(NT, dtype=jnp.int32)[None, :]
    cumulative = jnp.cumsum(starts, axis=1)
    padded = jnp.concatenate([jnp.zeros((starts.shape[0], WIN), jnp.float32), cumulative], axis=1)
    earlier = jnp.take_along_axis(padded, (slots - durations[:, None] + WIN).astype(jnp.int32), axis=1)
    return jax.ops.segment_sum(cumulative - earlier, tool_of_job, num_segments=K) / WIN

def window_adjoint(duals, tool_of_job, durations):
    slots = jnp.arange(NT, dtype=jnp.int32)[None, :]
    per_job = jnp.take(duals, tool_of_job, axis=0)
    padded = jnp.concatenate([per_job, jnp.zeros((per_job.shape[0], WIN), jnp.float32)], axis=1)
    suffix = lax.cumsum(padded, axis=1, reverse=True)
    later = jnp.take_along_axis(suffix, (slots + durations[:, None]).astype(jnp.int32), axis=1)
    return (suffix[:, :NT] - later) / WIN

def iterate(primal, dual_assign, dual_cap, adjoint_now, step_size, weight, cost, allowed, root, capacity_f, tool_of_job, durations):
    primal_step = step_size / weight
    dual_step = step_size * weight
    gradient = cost - dual_assign[:, None] / root + adjoint_now
    updated = jnp.where(allowed, jnp.maximum(primal - primal_step * gradient, 0.0), 0.0)
    extrapolated = 2.0 * updated - primal
    loads = window_loads(extrapolated, tool_of_job, durations)
    totals_new = lax.optimization_barrier(jnp.sum(updated, axis=1))
    totals_old = lax.optimization_barrier(jnp.sum(primal, axis=1))
    assign_next = dual_assign + dual_step * (root - (2.0 * totals_new - totals_old) / root)
    cap_next = jnp.maximum(dual_cap + dual_step * (loads - capacity_f), 0.0)
    return (updated, assign_next, cap_next, totals_new - totals_old)

def reference(start_density, assign_dual, cap_dual, tool_of_job, durations, releases, slack, capacity, job_weight, eta, omega):
    slots = jnp.arange(NT, dtype=jnp.int32)[None, :]
    span_end = slots + durations[:, None]
    allowed = (slots >= releases[:, None]) & (span_end <= NT)
    due_slot = releases + durations + slack
    lateness = jnp.maximum(span_end - due_slot[:, None], 0)
    cost = job_weight[:, None] * (span_end.astype(jnp.float32) / NT + lateness.astype(jnp.float32) / (4 * WIN))
    root = jnp.sqrt(jnp.float32(NT))
    weight = omega[0]
    step_size = eta[0]
    capacity_f = capacity.astype(jnp.float32)
    primal = jnp.where(allowed, start_density, 0.0)
    adjoint_first = window_adjoint(cap_dual, tool_of_job, durations)
    primal_one, assign_one, cap_one, delta_totals = iterate(primal, assign_dual, cap_dual, adjoint_first, step_size, weight, cost, allowed, root, capacity_f, tool_of_job, durations)
    adjoint_second = window_adjoint(cap_one, tool_of_job, durations)
    delta_primal = primal_one - primal
    delta_assign = assign_one - assign_dual
    delta_cap = cap_one - cap_dual
    movement = weight / 2.0 * jnp.sum(delta_primal * delta_primal) + (jnp.sum(delta_assign * delta_assign) + jnp.sum(delta_cap * delta_cap)) / (2.0 * weight)
    interaction = jnp.abs(jnp.sum(delta_primal * (adjoint_second - adjoint_first)) - jnp.sum(delta_assign * delta_totals) / root)
    step_next = movement / (interaction + movement / (1.5 * step_size))
    primal_two, assign_two, cap_two, unused = iterate(primal_one, assign_one, cap_one, adjoint_second, step_next, weight, cost, allowed, root, capacity_f, tool_of_job, durations)
    return (primal_two, assign_two, cap_two)
```

```python
import functools
import math
import types

import jax
import jax.numpy as jnp
from jax import lax
from jax.experimental import pallas as pl
from jax.experimental.pallas import tpu as pltpu
from jax.sharding import PartitionSpec as P

WIN = 32
LANES = 128
RING = 8
CORES = 2
F32, BF16 = jnp.float32, jnp.bfloat16
ORDER = (4, 3, 5, 2, 6, 1, 7, 0)
MESSAGES = 7


def window(x, dur, backward):
    n = x.shape[0]

    def move(v, k):
        return pltpu.roll(v, k if backward else n - k, 0)

    d = jnp.broadcast_to(dur, x.shape)
    span, total = 1, x
    acc = jnp.where((d & 1) != 0, x, 0.0)
    while span < WIN // 2:
        total = total + move(total, span)
        span *= 2
        acc = jnp.where((d & span) != 0, total + move(acc, span), acc)
    total = total + move(total, span)
    return jnp.where(d == WIN, total, acc)


def split(x):
    high = x.astype(BF16)
    return high, (x - high.astype(F32)).astype(BF16)


def dot(a, b, contract_b=0):
    return lax.dot_general(
        a, b, (((1,), (contract_b,)), ((), ())), preferred_element_type=F32
    )


def fold(x):
    return jnp.sum(x, axis=0, keepdims=True)


def scratch_of(rows, slots, tools, share, blocks, ny, nx):
    half = slots // 2
    dma, vmem = pltpu.SemaphoreType.DMA, pltpu.VMEM
    return dict(
        sd_v=vmem((rows, slots), F32),
        cap_v=vmem((tools, slots), F32),
        capac_v=vmem((share, slots), jnp.int32),
        cap_hi=vmem((tools, slots), BF16),
        cap_lo=vmem((tools, slots), BF16),
        mem=vmem((rows, tools), BF16),
        pj0=vmem((slots, rows), F32),
        pj1=vmem((slots, rows), F32),
        p0=vmem((slots, rows), F32),
        p1=vmem((slots, rows), F32),
        ex=vmem((slots, rows), F32),
        wdp=vmem((slots, rows), F32),
        grad=vmem((slots, rows), F32),
        ws=vmem((2 * slots, rows), BF16),
        hpj=vmem((2, WIN, rows), F32),
        hp=vmem((3, WIN, rows), F32),
        part=vmem((RING, CORES, slots, share), F32),
        pairbuf=vmem((2, RING, slots, share), F32),
        rsu=vmem((2, MESSAGES, half, share), F32),
        rsd=vmem((2, MESSAGES, half, share), F32),
        ag=vmem((RING, CORES, slots, share), F32),
        cap_s=vmem((slots, share), F32),
        capac_s=vmem((slots, share), F32),
        yrow=vmem((ny, 2 * blocks, LANES), F32),
        xrow=vmem((nx, 2 * blocks, LANES), F32),
        yrow2=vmem((ny, blocks, LANES), F32),
        xrow2=vmem((nx, blocks, LANES), F32),
        tot1=vmem((blocks, LANES), F32),
        a1=vmem((blocks, LANES), F32),
        accp=vmem((8, LANES), F32),
        sc_c=vmem((CORES, 8, LANES), F32),
        sc_z=vmem((RING, 8, LANES), F32),
        sc_y=vmem((ny, 8, LANES), F32),
        sc_x=vmem((nx, 8, LANES), F32),
        s_load=dma((3,)),
        s_out=dma((1,)),
        s_halo=dma((2, 5)),
        s_up=dma((2, 3, MESSAGES)),
        s_dn=dma((2, 3, MESSAGES)),
        s_pair=dma((2, 2, RING)),
        s_sib=dma((2, 2 * RING)),
        s_rowy=dma((2, 2, ny)),
        s_rowx=dma((2, 2, nx)),
        s_scc=dma((2, CORES)),
        s_scz=dma((2, RING)),
        s_scy=dma((2, ny)),
        s_scx=dma((2, nx)),
    )


def kernel(
    names, ny, nx, all_slots, sd, cap, capac, tool, dur, rel, slack, jw, assign, eta, omega,
    out_p, out_a, out_c, *scratch,
):
    r = types.SimpleNamespace(**dict(zip(names, scratch)))
    rows, slots = r.sd_v.shape
    tools, share = r.cap_v.shape[0], r.capac_v.shape[0]
    blocks, half, ntm = rows // LANES, slots // 2, ny * nx
    pair = CORES * share
    root = math.sqrt(all_slots)

    mj, mt = lax.axis_index("jobs"), lax.axis_index("tm")
    z, c = lax.div(mj, CORES), lax.rem(mj, CORES)
    x, y = lax.div(mt, ny), lax.rem(mt, ny)

    def zline(k):
        return lax.rem(z + k, RING) * CORES + c

    sibling = (z * CORES + 1 - c, mt)
    above, below = (zline(1), mt), (zline(RING - 1), mt)
    after, before = (mj, lax.rem(mt + 1, ntm)), (mj, lax.rem(mt + ntm - 1, ntm))
    z_peers = [(lax.rem(z + k, RING), (zline(k), mt)) for k in range(1, RING)]
    y_peers = [(lax.rem(y + k, ny), (mj, x * ny + lax.rem(y + k, ny))) for k in range(1, ny)]
    x_peers = [(lax.rem(x + k, nx), (mj, lax.rem(x + k, nx) * ny + y)) for k in range(1, nx)]

    sent = []

    def remote(src, dst, ssem, rsem, device):
        return pltpu.make_async_remote_copy(
            src_ref=src, dst_ref=dst, send_sem=ssem, recv_sem=rsem,
            device_id=device, device_id_type=pl.DeviceIdType.MESH,
        )

    def send(*args):
        copy = remote(*args)
        copy.start()
        sent.append(copy)

    def arrived(dst, ssem, rsem, device):
        remote(dst, dst, ssem, rsem, device).wait_recv()

    def drain():
        for copy in sent:
            copy.wait_send()
        sent.clear()

    def spread(buf, mine, peers, ssem, rsem):
        for k, (_, device) in enumerate(peers):
            send(buf.at[mine], buf.at[mine], ssem.at[k], rsem.at[mine], device)

        def wait():
            for k, (index, device) in enumerate(peers):
                arrived(buf.at[index], ssem.at[k], rsem.at[index], device)

        return wait

    def added(buf):
        total = buf[0]
        for k in range(1, buf.shape[0]):
            total = total + buf[k]
        return total

    first_tool = pl.multiple_of(mj * share, share)
    loads = [
        pltpu.make_async_copy(cap, r.cap_v, r.s_load.at[0]),
        pltpu.make_async_copy(sd, r.sd_v, r.s_load.at[1]),
        pltpu.make_async_copy(capac.at[pl.ds(first_tool, share), :], r.capac_v, r.s_load.at[2]),
    ]
    for copy in loads:
        copy.start()
    barrier = pltpu.get_barrier_semaphore()
    partners = [sibling, after, before]
    partners += [device for group in (z_peers, y_peers, x_peers) for _, device in group]
    for device in partners:
        pl.semaphore_signal(barrier, inc=1, device_id=device, device_id_type=pl.DeviceIdType.MESH)

    weight = omega[0]
    tau1, sigma1 = eta[0] / weight, eta[0] * weight

    lane = lax.broadcasted_iota(jnp.int32, (LANES, LANES), 1).astype(F32)

    @pl.loop(0, blocks)
    def _(b):
        row = jnp.broadcast_to(tool[pl.ds(b, 1), :].astype(F32), (LANES, LANES))
        column = row.T
        for k in range(tools // LANES):
            hit = jnp.where(column == lane + float(k * LANES), 1.0, 0.0).astype(BF16)
            r.mem[pl.ds(pl.multiple_of(b * LANES, LANES), LANES), k * LANES : (k + 1) * LANES] = hit

    loads[0].wait()

    @pl.loop(0, tools // share)
    def _(b):
        at = pl.ds(pl.multiple_of(b * share, share), share)
        high, low = split(r.cap_v[at, :])
        r.cap_hi[at, :] = high
        r.cap_lo[at, :] = low

    step = min(rows, 256)

    @pl.loop(0, rows // step)
    def _(b):
        at = pl.ds(pl.multiple_of(b * step, step), step)
        m = r.mem[at, :]
        found = dot(m, r.cap_hi[...]) + dot(m, r.cap_lo[...])
        r.pj0[:, at] = found.T

    def lanes_of(b):
        return pl.ds(pl.multiple_of(b * LANES, LANES), LANES)

    first_slot = mt * slots
    slot = lax.broadcasted_iota(jnp.int32, (slots, LANES), 0) + first_slot

    def allowed_of(b):
        return (slot >= rel[pl.ds(b, 1), :]) & (slot + dur[pl.ds(b, 1), :] <= all_slots)

    def cost_of(b):
        d = dur[pl.ds(b, 1), :]
        due = rel[pl.ds(b, 1), :] + d + slack[pl.ds(b, 1), :]
        end = slot + d
        late = jnp.maximum(end - due, 0)
        return jw[pl.ds(b, 1), :] * (
            end.astype(F32) * (1.0 / all_slots) + late.astype(F32) * (1.0 / (4 * WIN))
        )

    pl.semaphore_wait(barrier, len(partners))

    def halo(k, src, dst, device):
        send(src, dst, r.s_halo.at[0, k], r.s_halo.at[1, k], device)

    def halo_arrived(k, dst, device):
        arrived(dst, r.s_halo.at[0, k], r.s_halo.at[1, k], device)

    head, tail = pl.ds(0, WIN), pl.ds(slots - WIN, WIN)
    halo(0, r.pj0.at[head, :], r.hpj.at[0], before)

    loads[1].wait()

    @pl.loop(0, blocks)
    def _(b):
        start = r.sd_v[lanes_of(b), :].T
        p = jnp.where(allowed_of(b), start, 0.0)
        r.p0[:, lanes_of(b)] = p
        r.yrow[y, pl.ds(blocks + b, 1), :] = fold(p)

    halo(1, r.p0.at[tail, :], r.hp.at[0], after)

    loads[2].wait()
    r.cap_s[...] = r.cap_v[pl.ds(first_tool, share), :].T
    r.capac_s[...] = r.capac_v[...].astype(F32).T

    def extended(k, buf, b):
        below_rows = jnp.where(mt == ntm - 1, 0.0, r.hpj[k, :, lanes_of(b)])
        return jnp.concatenate([buf[:, lanes_of(b)], below_rows], axis=0)

    def preceded(k, buf, b):
        above_rows = jnp.where(mt == 0, 0.0, r.hp[k, :, lanes_of(b)])
        return jnp.concatenate([above_rows, buf[:, lanes_of(b)]], axis=0)

    halo_arrived(0, r.hpj.at[0], after)
    r.accp[...] = jnp.zeros_like(r.accp)

    @pl.loop(0, blocks)
    def _(b):
        d = dur[pl.ds(b, 1), :]
        adj = window(extended(0, r.pj0, b), d, False)[:slots] * (1.0 / WIN)
        p = r.p0[:, lanes_of(b)]
        gradient = cost_of(b) - assign[pl.ds(b, 1), :] * (1.0 / root) + adj
        new = jnp.where(allowed_of(b), jnp.maximum(p - tau1 * gradient, 0.0), 0.0)
        r.p1[:, lanes_of(b)] = new
        r.ex[:, lanes_of(b)] = 2.0 * new - p
        r.yrow[y, pl.ds(b, 1), :] = fold(new)
        moved = new - p
        r.accp[0:1, :] += fold(moved * moved)

    halo(2, r.ex.at[tail, :], r.hp.at[1], after)
    rows_y = spread(r.yrow, y, y_peers, r.s_rowy.at[0, 0], r.s_rowy.at[0, 1])

    halo_arrived(1, r.hp.at[0], before)

    @pl.loop(0, blocks)
    def _(b):
        d = dur[pl.ds(b, 1), :]
        r.wdp[:, lanes_of(b)] = window(preceded(0, r.p0, b), d, True)[WIN:]

    halo_arrived(2, r.hp.at[1], before)

    @pl.loop(0, blocks)
    def _(b):
        d = dur[pl.ds(b, 1), :]
        w = window(preceded(1, r.ex, b), d, True)[WIN:]
        r.wdp[:, lanes_of(b)] = 0.5 * (w - r.wdp[:, lanes_of(b)])
        high, low = split(w)
        r.ws[0:slots, lanes_of(b)] = high
        r.ws[slots : 2 * slots, lanes_of(b)] = low

    def reduced_loads(it, extra):
        paired = set()

        def produce(i):
            owner = lax.rem(z + ORDER[i], RING)
            full = dot(r.ws[...], r.mem[:, pl.ds(pl.multiple_of(owner * pair, pair), pair)])
            full = (full[:slots] + full[slots:]) * (1.0 / WIN)
            r.part[i, 0] = full[:, :share]
            r.part[i, 1] = full[:, share:]
            send(r.part.at[i, 1 - c], r.pairbuf.at[it, i], r.s_pair.at[it, 0, i], r.s_pair.at[it, 1, i], sibling)

        def mine(i, side):
            if i not in paired:
                arrived(r.pairbuf.at[it, i], r.s_pair.at[it, 0, i], r.s_pair.at[it, 1, i], sibling)
                paired.add(i)
            at = pl.ds(side * half, half)
            return r.part[i, c, at, :] + r.pairbuf[it, i, at, :]

        def message(m, upward):
            buf, sems = (r.rsu, r.s_up) if upward else (r.rsd, r.s_dn)
            to, source = (above, below) if upward else (below, above)
            distance = 4 - (m + 1) // 2
            i = ORDER.index(distance if upward else RING - distance)
            side = m % 2 if upward else 1 - m % 2
            value = mine(i, side)
            if m >= 2:
                arrived(buf.at[it, m - 2], sems.at[it, 0, m - 2], sems.at[it, 1, m - 2], source)
                value = value + buf[it, m - 2]
            at = pl.ds(side * half, half)
            r.part[i, c, at, :] = value
            send(r.part.at[i, c, at, :], buf.at[it, m], sems.at[it, 0, m], sems.at[it, 1, m], to)

        ready = {0: 3, 1: 5, 2: 7, 3: 8}
        done = 0
        for m in range(MESSAGES):
            while done < ready.get(m, RING):
                produce(done)
                done += 1
            message(m, True)
            message(m, False)
            extra(m)
        out = []
        own = ORDER.index(0)
        for side in (0, 1):
            value = mine(own, side)
            for upward, buf, sems, source in ((True, r.rsu, r.s_up, below), (False, r.rsd, r.s_dn, above)):
                m = 6 - side if upward else 5 + side
                arrived(buf.at[it, m], sems.at[it, 0, m], sems.at[it, 1, m], source)
                value = value + buf[it, m]
            out.append(value)
        return jnp.concatenate(out, axis=0)

    def rows_first(m):
        if m == 1:
            rows_y()
            r.xrow[x] = added(r.yrow)
            rows_first.wait = spread(r.xrow, x, x_peers, r.s_rowx.at[0, 0], r.s_rowx.at[0, 1])
        if m == 4:
            rows_first.wait()
            total = added(r.xrow)
            new, old = total[:blocks], total[blocks:]
            r.tot1[...] = new
            delta = sigma1 * (root - (2.0 * new - old) * (1.0 / root))
            r.a1[...] = assign[...] + delta
            lead = jnp.where(mt == 0, 1.0, 0.0)
            r.accp[3:4, :] = lead * fold(delta * delta)
            r.accp[4:5, :] = lead * fold(delta * (new - old))

    loads1 = reduced_loads(0, rows_first)
    cap1 = jnp.maximum(r.cap_s[...] + sigma1 * (loads1 - r.capac_s[...]), 0.0)
    delta_cap = cap1 - r.cap_s[...]
    r.accp[1:2, :] = fold(delta_cap * delta_cap)
    r.ag[z, c] = cap1
    drain()

    def part_of(hops, side):
        return (lax.rem(z + hops + RING, RING), c, pl.ds(side * half, half), slice(None))

    def pass_on(m, upward):
        sems, to = (r.s_up, above) if upward else (r.s_dn, below)
        hops = -(m // 2) if upward else m // 2
        at = part_of(hops, m % 2 if upward else 1 - m % 2)
        send(r.ag.at[at], r.ag.at[at], sems.at[0, 2, m], sems.at[1, 2, m], to)

    def across(hops, side):
        k = 2 * (hops % RING) + side
        at = part_of(hops, side)
        send(r.ag.at[at], r.ag.at[at], r.s_sib.at[0, k], r.s_sib.at[1, k], sibling)

    def crossed(hops, side):
        k = 2 * (hops % RING) + side
        at = (lax.rem(z + hops + RING, RING), 1 - c, pl.ds(side * half, half), slice(None))
        arrived(r.ag.at[at], r.s_sib.at[0, k], r.s_sib.at[1, k], sibling)

    def gather(hops, first=False):
        crossed(hops, 0)
        crossed(hops, 1)
        owner = lax.rem(z + hops + RING, RING)
        high, low = split(jnp.concatenate([r.ag[owner, 0], r.ag[owner, 1]], axis=1))
        both = jnp.concatenate([high, low], axis=0)
        full = dot(both, r.mem[:, pl.ds(pl.multiple_of(owner * pair, pair), pair)], 1)
        full = full[:slots] + full[slots:]
        r.pj1[...] = full if first else r.pj1[...] + full

    for m in (0, 1):
        pass_on(m, True)
        pass_on(m, False)
    across(0, 0)
    across(0, 1)
    work = {0: (0,), 2: (-1,), 3: (1,), 4: (-2,), 5: (2,), 6: (-3, 3)}
    for m in range(MESSAGES):
        for upward in (True, False):
            hops = -1 - m // 2 if upward else 1 + m // 2
            side = m % 2 if upward else 1 - m % 2
            sems, source = (r.s_up, below) if upward else (r.s_dn, above)
            arrived(r.ag.at[part_of(hops, side)], sems.at[0, 2, m], sems.at[1, 2, m], source)
            if m + 2 < MESSAGES:
                pass_on(m + 2, upward)
            across(hops, side)
        for hops in work.get(m, ()):
            gather(hops, first=hops == 0)
    gather(4)

    halo(3, r.pj1.at[head, :], r.hpj.at[1], before)

    @pl.loop(0, blocks)
    def _(b):
        at = lanes_of(b)
        r.accp[2:3, :] += fold((r.pj1[:, at] - r.pj0[:, at]) * r.wdp[:, at]) * (1.0 / WIN)

    r.sc_c[c] = r.accp[...]
    wait = spread(r.sc_c, c, [(1 - c, sibling)], r.s_scc.at[0], r.s_scc.at[1])
    wait()
    r.sc_z[z] = added(r.sc_c)
    wait = spread(r.sc_z, z, z_peers, r.s_scz.at[0], r.s_scz.at[1])
    halo_arrived(3, r.hpj.at[1], after)

    def second_gradient(b):
        d = dur[pl.ds(b, 1), :]
        adj = window(extended(1, r.pj1, b), d, False)[:slots] * (1.0 / WIN)
        r.grad[:, lanes_of(b)] = cost_of(b) - r.a1[pl.ds(b, 1), :] * (1.0 / root) + adj

    third = max(blocks // 3, 1)
    pl.loop(0, third)(second_gradient)
    wait()
    r.sc_y[y] = added(r.sc_z)
    wait = spread(r.sc_y, y, y_peers, r.s_scy.at[0], r.s_scy.at[1])
    pl.loop(third, 2 * third)(second_gradient)
    wait()
    r.sc_x[x] = added(r.sc_y)
    wait = spread(r.sc_x, x, x_peers, r.s_scx.at[0], r.s_scx.at[1])
    if blocks > 2 * third:
        pl.loop(2 * third, blocks)(second_gradient)
    wait()
    sums = jnp.sum(added(r.sc_x), axis=1, keepdims=True)
    sum_primal, sum_cap, cross_primal, sum_assign, cross_assign = (sums[k : k + 1] for k in range(5))
    movement = weight * 0.5 * sum_primal + (sum_assign + sum_cap) / (2.0 * weight)
    interaction = jnp.abs(cross_primal - cross_assign * (1.0 / root))
    step_next = movement / (interaction + movement / (1.5 * eta[0]))
    tau2 = jnp.broadcast_to(step_next / weight, (1, LANES))
    sigma2 = jnp.broadcast_to(step_next * weight, (1, LANES))

    @pl.loop(0, blocks)
    def _(b):
        at = lanes_of(b)
        p = r.p1[:, at]
        new = jnp.where(allowed_of(b), jnp.maximum(p - tau2 * r.grad[:, at], 0.0), 0.0)
        r.p0[:, at] = new
        r.ex[:, at] = 2.0 * new - p
        r.yrow2[y, pl.ds(b, 1), :] = fold(new)

    drain()
    halo(4, r.ex.at[tail, :], r.hp.at[2], after)
    rows2_y = spread(r.yrow2, y, y_peers, r.s_rowy.at[1, 0], r.s_rowy.at[1, 1])

    @pl.loop(0, blocks)
    def _(b):
        r.sd_v[lanes_of(b), :] = r.p0[:, lanes_of(b)].T

    store = pltpu.make_async_copy(r.sd_v, out_p, r.s_out.at[0])
    store.start()
    halo_arrived(4, r.hp.at[2], before)

    @pl.loop(0, blocks)
    def _(b):
        d = dur[pl.ds(b, 1), :]
        high, low = split(window(preceded(2, r.ex, b), d, True)[WIN:])
        r.ws[0:slots, lanes_of(b)] = high
        r.ws[slots : 2 * slots, lanes_of(b)] = low

    def rows_second(m):
        if m == 1:
            rows2_y()
            r.xrow2[x] = added(r.yrow2)
            rows_second.wait = spread(r.xrow2, x, x_peers, r.s_rowx.at[1, 0], r.s_rowx.at[1, 1])
        if m == 4:
            rows_second.wait()
            new = added(r.xrow2)
            out_a[...] = r.a1[...] + sigma2 * (root - (2.0 * new - r.tot1[...]) * (1.0 / root))

    loads2 = reduced_loads(1, rows_second)
    cap2 = jnp.maximum(r.ag[z, c] + sigma2 * (loads2 - r.capac_s[...]), 0.0)
    out_c[...] = cap2.T
    drain()
    store.wait()


def shards(sizes, all_slots, start, assign, cap, tool, dur, rel, slack, capac, jw, eta, omega):
    ny, nx = sizes
    rows, slots = start.shape
    tools = cap.shape[0]
    share = tools // (RING * CORES)
    blocks = rows // LANES
    scratch = scratch_of(rows, slots, tools, share, blocks, ny, nx)
    hbm = pl.BlockSpec(memory_space=pl.ANY)
    vec = pl.BlockSpec(memory_space=pltpu.VMEM)
    smem = pl.BlockSpec(memory_space=pltpu.SMEM)

    def tiles(v):
        return v.reshape(blocks, LANES)

    p, a, c = pl.pallas_call(
        functools.partial(kernel, tuple(scratch), ny, nx, all_slots),
        out_shape=(
            jax.ShapeDtypeStruct((rows, slots), F32),
            jax.ShapeDtypeStruct((blocks, LANES), F32),
            jax.ShapeDtypeStruct((share, slots), F32),
        ),
        in_specs=[hbm, hbm, hbm] + [vec] * 6 + [smem] * 2,
        out_specs=(hbm, vec, vec),
        scratch_shapes=list(scratch.values()),
        compiler_params=pltpu.CompilerParams(
            collective_id=0, has_side_effects=True, vmem_limit_bytes=56 * 1024 * 1024
        ),
        cost_estimate=pl.CostEstimate(flops=8_600_000_000, bytes_accessed=6_000_000, transcendentals=0),
        name="pdhg",
    )(start, cap, capac, *map(tiles, (tool, dur, rel, slack, jw, assign)), eta, omega)
    return p, a.reshape(rows), c


def solution(mesh):
    ntm = mesh.shape["tm"]
    ny = 4 if ntm >= 16 else ntm

    def run(start, *rest):
        body = functools.partial(shards, (ny, ntm // ny), start.shape[1])
        return jax.shard_map(
            body,
            mesh=mesh,
            in_specs=(
                P("jobs", "tm"), P("jobs"), P(None, "tm"), P("jobs"), P("jobs"), P("jobs"),
                P("jobs"), P(None, "tm"), P("jobs"), P(), P(),
            ),
            out_specs=(P("jobs", "tm"), P("jobs"), P("jobs", "tm")),
            check_vma=False,
        )(start, *rest)

    return run
```

```python
import functools
import math
import types

import jax
import jax.numpy as jnp
from jax import lax
from jax.experimental import pallas as pl
from jax.experimental.pallas import tpu as pltpu
from jax.sharding import PartitionSpec as P

WIN = 32
LANES = 128
RING = 8
CORES = 2
F32, BF16 = jnp.float32, jnp.bfloat16
ORDER = (4, 3, 5, 2, 6, 1, 7, 0)
MESSAGES = 7
PIECES = 2


def window(x, dur, backward):
    n = x.shape[0]

    def move(v, k):
        return pltpu.roll(v, k if backward else n - k, 0)

    d = jnp.broadcast_to(dur, x.shape)
    span, total = 1, x
    acc = jnp.where((d & 1) != 0, x, 0.0)
    while span < WIN // 2:
        total = total + move(total, span)
        span *= 2
        acc = jnp.where((d & span) != 0, total + move(acc, span), acc)
    total = total + move(total, span)
    return jnp.where(d == WIN, total, acc)


def split(x):
    high = x.astype(BF16)
    return high, (x - high.astype(F32)).astype(BF16)


def dot(a, b, contract_b=0):
    return lax.dot_general(
        a, b, (((1,), (contract_b,)), ((), ())), preferred_element_type=F32
    )


def fold(x):
    return jnp.sum(x, axis=0, keepdims=True)


def scratch_of(rows, slots, tools, share, blocks, ny, nx):
    piece = slots // (2 * PIECES)
    dma, vmem = pltpu.SemaphoreType.DMA, pltpu.VMEM
    return dict(
        ints=vmem((4, blocks, LANES), jnp.int32),
        floats=vmem((2, blocks, LANES), F32),
        eta=pltpu.SMEM((1,), F32),
        omega=pltpu.SMEM((1,), F32),
        sd_v=vmem((rows, slots), F32),
        cap_v=vmem((tools, slots), F32),
        capac_v=vmem((share, slots), jnp.int32),
        cap_hi=vmem((tools, slots), BF16),
        cap_lo=vmem((tools, slots), BF16),
        mem=vmem((rows, tools), BF16),
        pj0=vmem((slots + 2 * WIN, rows), F32),
        pj1=vmem((slots + 2 * WIN, rows), F32),
        p0=vmem((slots + WIN, rows), F32),
        p1=vmem((slots + WIN, rows), F32),
        grad=vmem((slots + WIN, rows), F32),
        wdp=vmem((slots, rows), F32),
        ws=vmem((2 * slots, rows), BF16),
        part=vmem((RING, CORES, slots, share), F32),
        pairbuf=vmem((2, RING, slots, share), F32),
        rsu=vmem((2, MESSAGES, PIECES, piece, share), F32),
        rsd=vmem((2, MESSAGES, PIECES, piece, share), F32),
        ag=vmem((RING, CORES, slots, share), F32),
        cap_s=vmem((slots, share), F32),
        capac_s=vmem((slots, share), F32),
        c2=vmem((slots, share), F32),
        yrow=vmem((ny, 2 * blocks, LANES), F32),
        xrow=vmem((nx, 2 * blocks, LANES), F32),
        yrow2=vmem((ny, blocks, LANES), F32),
        xrow2=vmem((nx, blocks, LANES), F32),
        tot1=vmem((blocks, LANES), F32),
        a1=vmem((blocks, LANES), F32),
        accp=vmem((8, LANES), F32),
        sc_c=vmem((CORES, 8, LANES), F32),
        sc_z=vmem((RING, 8, LANES), F32),
        sc_t=vmem((ny * nx, 8, LANES), F32),
        s_load=dma((11,)),
        s_out=dma((1,)),
        s_halo=dma((2, 5)),
        s_up=dma((2, 3, MESSAGES, PIECES)),
        s_dn=dma((2, 3, MESSAGES, PIECES)),
        s_pair=dma((2, 2, RING)),
        s_sib=dma((2, 2 * RING)),
        s_rowy=dma((2, 2, ny)),
        s_rowx=dma((2, 2, nx)),
        s_scc=dma((2, CORES)),
        s_scz=dma((2, RING)),
        s_sct=dma((2, ny * nx)),
    )


def kernel(
    names, ny, nx, all_slots, sd, cap, capac, tool_in, dur_in, rel_in, slack_in, jw_in, assign_in,
    eta_in, omega_in, out_p, out_a, out_c, *scratch,
):
    r = types.SimpleNamespace(**dict(zip(names, scratch)))
    rows, slots = r.sd_v.shape
    tools, share = r.cap_v.shape[0], r.capac_v.shape[0]
    blocks, half, ntm = rows // LANES, slots // 2, ny * nx
    piece = half // PIECES
    pair = CORES * share
    root = math.sqrt(all_slots)

    mj, mt = lax.axis_index("jobs"), lax.axis_index("tm")
    z, c = lax.div(mj, CORES), lax.rem(mj, CORES)
    x, y = lax.div(mt, ny), lax.rem(mt, ny)

    def zline(k):
        return lax.rem(z + k, RING) * CORES + c

    sibling = (z * CORES + 1 - c, mt)
    above, below = (zline(1), mt), (zline(RING - 1), mt)
    after, before = (mj, lax.rem(mt + 1, ntm)), (mj, lax.rem(mt + ntm - 1, ntm))
    z_peers = [(lax.rem(z + k, RING), (zline(k), mt)) for k in range(1, RING)]
    y_peers = [(lax.rem(y + k, ny), (mj, x * ny + lax.rem(y + k, ny))) for k in range(1, ny)]
    x_peers = [(lax.rem(x + k, nx), (mj, lax.rem(x + k, nx) * ny + y)) for k in range(1, nx)]

    t_peers = [(lax.rem(mt + k, ntm), (mj, lax.rem(mt + k, ntm))) for k in range(1, ntm)]
    tool, dur, rel, slack = (r.ints.at[k] for k in range(4))
    jw, assign = (r.floats.at[k] for k in range(2))

    sent = []

    def remote(src, dst, ssem, rsem, device):
        return pltpu.make_async_remote_copy(
            src_ref=src, dst_ref=dst, send_sem=ssem, recv_sem=rsem,
            device_id=device, device_id_type=pl.DeviceIdType.MESH,
        )

    def send(*args):
        copy = remote(*args)
        copy.start()
        sent.append(copy)

    def arrived(dst, ssem, rsem, device):
        remote(dst, dst, ssem, rsem, device).wait_recv()

    def drain():
        for copy in sent:
            copy.wait_send()
        sent.clear()

    def spread(buf, mine, peers, ssem, rsem):
        for k, (_, device) in enumerate(peers):
            send(buf.at[mine], buf.at[mine], ssem.at[k], rsem.at[mine], device)

        def wait():
            for k, (index, device) in enumerate(peers):
                arrived(buf.at[index], ssem.at[k], rsem.at[index], device)

        return wait

    def added(buf):
        total = buf[0]
        for k in range(1, buf.shape[0]):
            total = total + buf[k]
        return total

    barrier = pltpu.get_barrier_semaphore()
    partners = [sibling, above, below, before, after]
    partners += [device for group in (y_peers, x_peers) for _, device in group]
    for device in partners:
        pl.semaphore_signal(barrier, inc=1, device_id=device, device_id_type=pl.DeviceIdType.MESH)
    first_tool = pl.multiple_of(mj * share, share)
    loads = [
        pltpu.make_async_copy(source, target, r.s_load.at[k])
        for k, (source, target) in enumerate(
            [
                (tool_in, tool), (cap, r.cap_v), (sd, r.sd_v), (dur_in, dur), (rel_in, rel), (slack_in, slack),
                (jw_in, jw), (assign_in, assign), (eta_in, r.eta), (omega_in, r.omega),
                (capac.at[pl.ds(first_tool, share), :], r.capac_v),
            ]
        )
    ]
    for copy in loads:
        copy.start()
    loads[0].wait()

    lane = lax.broadcasted_iota(jnp.int32, (LANES, LANES), 1).astype(F32)

    @pl.loop(0, blocks)
    def _(b):
        row = jnp.broadcast_to(tool[pl.ds(b, 1), :].astype(F32), (LANES, LANES))
        column = row.T
        for k in range(tools // LANES):
            hit = jnp.where(column == lane + float(k * LANES), 1.0, 0.0).astype(BF16)
            r.mem[pl.ds(pl.multiple_of(b * LANES, LANES), LANES), k * LANES : (k + 1) * LANES] = hit

    loads[1].wait()

    @pl.loop(0, tools // share)
    def _(b):
        at = pl.ds(pl.multiple_of(b * share, share), share)
        high, low = split(r.cap_v[at, :])
        r.cap_hi[at, :] = high
        r.cap_lo[at, :] = low

    step = min(rows, 256)

    @pl.loop(0, rows // step)
    def _(b):
        at = pl.ds(pl.multiple_of(b * step, step), step)
        m = r.mem[at, :]
        found = dot(m, r.cap_hi[...]) + dot(m, r.cap_lo[...])
        r.pj0[WIN : WIN + slots, at] = found.T

    def lanes_of(b):
        return pl.ds(pl.multiple_of(b * LANES, LANES), LANES)

    slot = lax.broadcasted_iota(jnp.int32, (slots + WIN, LANES), 0) + (mt * slots - WIN)
    own = slice(WIN, WIN + slots)

    def allowed_of(b, s=slot):
        return (s >= rel[pl.ds(b, 1), :]) & (s + dur[pl.ds(b, 1), :] <= all_slots)

    def cost_of(b, s=slot):
        d = dur[pl.ds(b, 1), :]
        due = rel[pl.ds(b, 1), :] + d + slack[pl.ds(b, 1), :]
        end = s + d
        late = jnp.maximum(end - due, 0)
        return jw[pl.ds(b, 1), :] * (
            end.astype(F32) * (1.0 / all_slots) + late.astype(F32) * (1.0 / (4 * WIN))
        )

    for copy in loads[2:]:
        copy.wait()
    weight, eta = r.omega[0], r.eta[0]
    tau1, sigma1 = eta / weight, eta * weight

    @pl.loop(0, blocks)
    def _(b):
        start = r.sd_v[lanes_of(b), :].T
        p = jnp.where(allowed_of(b, slot[WIN:]), start, 0.0)
        r.p0[own, lanes_of(b)] = p
        r.yrow[y, pl.ds(blocks + b, 1), :] = fold(p)

    pl.semaphore_wait(barrier, len(partners))

    def halo(k, src, dst, device):
        send(src, dst, r.s_halo.at[0, k], r.s_halo.at[1, k], device)

    def halo_arrived(k, dst, device):
        arrived(dst, r.s_halo.at[0, k], r.s_halo.at[1, k], device)

    lead, head = pl.ds(0, WIN), pl.ds(WIN, WIN)
    tail, beyond = pl.ds(slots, WIN), pl.ds(slots + WIN, WIN)

    def exchange(k, buf):
        halo(k, buf.at[head, :], buf.at[beyond, :], before)
        halo(k + 1, buf.at[tail, :], buf.at[lead, :], after)

        def wait():
            halo_arrived(k, buf.at[beyond, :], after)
            halo_arrived(k + 1, buf.at[lead, :], before)

        return wait

    duals_wait = exchange(0, r.pj0)
    halo(2, r.p0.at[tail, :], r.p0.at[lead, :], after)

    r.cap_s[...] = r.cap_v[pl.ds(first_tool, share), :].T
    r.capac_s[...] = r.capac_v[...].astype(F32).T

    def adjoint(buf, b):
        at = lanes_of(b)
        past = jnp.where(mt == ntm - 1, 0.0, buf[beyond, at])
        x = jnp.concatenate([buf[0 : slots + WIN, at], past], axis=0)
        return window(x, dur[pl.ds(b, 1), :], False)[: slots + WIN] * (1.0 / WIN)

    def loaded(x, b):
        return window(x, dur[pl.ds(b, 1), :], True)[WIN:]

    def keep(w, b, first=0):
        high, low = split(w)
        n = w.shape[0]
        r.ws[first : first + n, lanes_of(b)] = high
        r.ws[slots + first : slots + first + n, lanes_of(b)] = low

    inner = slice(WIN, slots)
    r.accp[...] = jnp.zeros_like(r.accp)

    def updated(b, s, p, adj):
        gradient = cost_of(b, s) - assign[pl.ds(b, 1), :] * (1.0 / root) + adj * (1.0 / WIN)
        return jnp.where(allowed_of(b, s), jnp.maximum(p - tau1 * gradient, 0.0), 0.0)

    @pl.loop(0, blocks)
    def _(b):
        at = lanes_of(b)
        p = r.p0[inner, at]
        adj = window(r.pj0[own, at], dur[pl.ds(b, 1), :], False)[: slots - WIN]
        new = updated(b, slot[inner], p, adj)
        r.p1[inner, at] = new
        r.yrow[y, pl.ds(b, 1), :] = fold(new)
        moved = new - p
        r.accp[0:1, :] += fold(moved * moved)
        w = loaded(2.0 * new - p, b)
        r.wdp[WIN : slots - WIN, at] = 0.5 * (w - loaded(p, b))
        keep(w, b, WIN)

    duals_wait()
    halo_arrived(2, r.p0.at[lead, :], before)
    low, high = slice(0, WIN), slice(2 * WIN, 3 * WIN)
    edges = jnp.concatenate([slot[:WIN], slot[slots:]], axis=0)

    @pl.loop(0, blocks)
    def _(b):
        at = lanes_of(b)
        past = jnp.where(mt == ntm - 1, 0.0, r.pj0[beyond, at])
        bands = jnp.concatenate([r.pj0[: 2 * WIN, at], r.pj0[tail, at], past], axis=0)
        adj = window(bands, dur[pl.ds(b, 1), :], False)
        adj = jnp.concatenate([adj[low], adj[high]], axis=0)
        p = jnp.concatenate([r.p0[lead, at], r.p0[tail, at]], axis=0)
        p = jnp.where(allowed_of(b, edges), p, 0.0)
        new = updated(b, edges, p, adj)
        r.p1[lead, at] = new[:WIN]
        r.p1[tail, at] = new[WIN:]
        r.yrow[y, pl.ds(b, 1), :] += fold(new[WIN:])
        moved = (new - p)[WIN:]
        r.accp[0:1, :] += fold(moved * moved)
        inside = pl.ds(slots - WIN, WIN)
        old = jnp.concatenate([p[:WIN], r.p0[head, at], r.p0[inside, at], p[WIN:]], axis=0)
        now = jnp.concatenate([new[:WIN], r.p1[head, at], r.p1[inside, at], new[WIN:]], axis=0)
        w, v = (window(x, dur[pl.ds(b, 1), :], True) for x in (2.0 * now - old, old))
        for first, k in ((0, WIN), (slots - WIN, 3 * WIN)):
            r.wdp[first : first + WIN, at] = 0.5 * (w[k : k + WIN] - v[k : k + WIN])
            keep(w[k : k + WIN], b, first)

    rows_y = spread(r.yrow, y, y_peers, r.s_rowy.at[0, 0], r.s_rowy.at[0, 1])

    def rows_of(side, q):
        return pl.ds(side * half + q * piece, piece)

    def reduced_loads(it, extra, finish):
        paired = set()

        def produce(i):
            owner = lax.rem(z + ORDER[i], RING)
            full = dot(r.ws[...], r.mem[:, pl.ds(pl.multiple_of(owner * pair, pair), pair)])
            full = (full[:slots] + full[slots:]) * (1.0 / WIN)
            r.part[i, 0] = full[:, :share]
            r.part[i, 1] = full[:, share:]
            send(r.part.at[i, 1 - c], r.pairbuf.at[it, i], r.s_pair.at[it, 0, i], r.s_pair.at[it, 1, i], sibling)

        def mine(i, side, q):
            if i not in paired:
                arrived(r.pairbuf.at[it, i], r.s_pair.at[it, 0, i], r.s_pair.at[it, 1, i], sibling)
                paired.add(i)
            at = rows_of(side, q)
            return r.part[i, c, at, :] + r.pairbuf[it, i, at, :]

        def incoming(upward, m, q):
            buf, sems, source = (r.rsu, r.s_up, below) if upward else (r.rsd, r.s_dn, above)
            arrived(buf.at[it, m, q], sems.at[it, 0, m, q], sems.at[it, 1, m, q], source)
            return buf[it, m, q]

        def message(m, q, upward):
            buf, sems, to = (r.rsu, r.s_up, above) if upward else (r.rsd, r.s_dn, below)
            distance = 4 - (m + 1) // 2
            i = ORDER.index(distance if upward else RING - distance)
            side = m % 2 if upward else 1 - m % 2
            value = mine(i, side, q)
            if m >= 2:
                value = value + incoming(upward, m - 2, q)
            at = rows_of(side, q)
            r.part[i, c, at, :] = value
            send(r.part.at[i, c, at, :], buf.at[it, m, q], sems.at[it, 0, m, q], sems.at[it, 1, m, q], to)

        ready = {0: 3, 1: 3, 2: 5, 3: 5, 4: 7, 5: 7}
        done = 0
        for m in range(MESSAGES):
            while done < ready.get(m, RING):
                produce(done)
                done += 1
            for q in range(PIECES):
                message(m, q, True)
                message(m, q, False)
            extra(m)
        i = ORDER.index(0)
        for q in range(PIECES):
            for side in (0, 1):
                value = mine(i, side, q) + incoming(True, 6 - side, q) + incoming(False, 5 + side, q)
                finish(side, q, rows_of(side, q), value)

    def rows_first(m):
        if m == 3:
            rows_y()
            r.xrow[x] = added(r.yrow)
            rows_first.wait = spread(r.xrow, x, x_peers, r.s_rowx.at[0, 0], r.s_rowx.at[0, 1])
        if m == MESSAGES + 1:
            rows_first.wait()
            total = added(r.xrow)
            new, old = total[:blocks], total[blocks:]
            r.tot1[...] = new
            delta = sigma1 * (root - (2.0 * new - old) * (1.0 / root))
            r.a1[...] = assign[...] + delta
            once = jnp.where(mt == 0, 1.0, 0.0)
            r.accp[3:4, :] = once * fold(delta * delta)
            r.accp[4:5, :] = once * fold(delta * (new - old))

    def part_of(hops, side, q=None):
        at = pl.ds(side * half, half) if q is None else rows_of(side, q)
        return (lax.rem(z + hops + RING, RING), c, at, slice(None))

    def pass_on(m, q, upward):
        sems, to = (r.s_up, above) if upward else (r.s_dn, below)
        hops = -(m // 2) if upward else m // 2
        at = part_of(hops, m % 2 if upward else 1 - m % 2, q)
        send(r.ag.at[at], r.ag.at[at], sems.at[0, 2, m, q], sems.at[1, 2, m, q], to)

    def across(hops, side):
        k = 2 * (hops % RING) + side
        at = part_of(hops, side)
        send(r.ag.at[at], r.ag.at[at], r.s_sib.at[0, k], r.s_sib.at[1, k], sibling)

    def finish_first(side, q, at, value):
        old = r.cap_s[at, :]
        new = jnp.maximum(old + sigma1 * (value - r.capac_s[at, :]), 0.0)
        r.ag[z, c, at, :] = new
        pass_on(side, q, True)
        pass_on(1 - side, q, False)
        moved = new - old
        r.accp[1:2, :] += fold(moved * moved)
        if q == PIECES - 1:
            across(0, side)

    reduced_loads(0, rows_first, finish_first)

    def crossed(hops, side):
        k = 2 * (hops % RING) + side
        at = (lax.rem(z + hops + RING, RING), 1 - c, pl.ds(side * half, half), slice(None))
        arrived(r.ag.at[at], r.s_sib.at[0, k], r.s_sib.at[1, k], sibling)

    def gather(hops, first=False):
        crossed(hops, 0)
        crossed(hops, 1)
        owner = lax.rem(z + hops + RING, RING)
        high, low = split(jnp.concatenate([r.ag[owner, 0], r.ag[owner, 1]], axis=1))
        both = jnp.concatenate([high, low], axis=0)
        full = dot(both, r.mem[:, pl.ds(pl.multiple_of(owner * pair, pair), pair)], 1)
        full = full[:slots] + full[slots:]
        r.pj1[own, :] = full if first else r.pj1[own, :] + full

    work = {1: (0,), 3: (-1, 1), 5: (-2, 2), 6: (-3, 3)}
    for m in range(MESSAGES):
        for upward in (True, False):
            hops = -1 - m // 2 if upward else 1 + m // 2
            side = m % 2 if upward else 1 - m % 2
            sems, source = (r.s_up, below) if upward else (r.s_dn, above)
            for q in range(PIECES):
                arrived(r.ag.at[part_of(hops, side, q)], sems.at[0, 2, m, q], sems.at[1, 2, m, q], source)
                if m + 2 < MESSAGES:
                    pass_on(m + 2, q, upward)
            across(hops, side)
        for hops in work.get(m, ()):
            gather(hops, first=hops == 0)
        rows_first(MESSAGES + m)
    gather(4)

    duals_wait = exchange(3, r.pj1)

    @pl.loop(0, blocks)
    def _(b):
        at = lanes_of(b)
        r.accp[2:3, :] += fold((r.pj1[own, at] - r.pj0[own, at]) * r.wdp[:, at]) * (1.0 / WIN)

    r.sc_c[c] = r.accp[...]
    spread(r.sc_c, c, [(1 - c, sibling)], r.s_scc.at[0], r.s_scc.at[1])()
    r.sc_z[z] = added(r.sc_c)
    sums_wait = spread(r.sc_z, z, z_peers, r.s_scz.at[0], r.s_scz.at[1])
    sums_wait()
    r.sc_t[mt] = added(r.sc_z)
    sums_wait = spread(r.sc_t, mt, t_peers, r.s_sct.at[0], r.s_sct.at[1])
    duals_wait()

    @pl.loop(0, blocks)
    def _(b):
        r.grad[:, lanes_of(b)] = cost_of(b) - r.a1[pl.ds(b, 1), :] * (1.0 / root) + adjoint(r.pj1, b)

    sums_wait()
    sums = jnp.sum(added(r.sc_t), axis=1, keepdims=True)
    sum_primal, sum_cap, cross_primal, sum_assign, cross_assign = (sums[k : k + 1] for k in range(5))
    movement = weight * 0.5 * sum_primal + (sum_assign + sum_cap) / (2.0 * weight)
    interaction = jnp.abs(cross_primal - cross_assign * (1.0 / root))
    step_next = movement / (interaction + movement / (1.5 * eta))
    tau2 = jnp.broadcast_to(step_next / weight, (1, LANES))
    sigma2 = jnp.broadcast_to(step_next * weight, (1, LANES))

    drain()

    @pl.loop(0, blocks)
    def _(b):
        at = lanes_of(b)
        p = r.p1[:, at]
        new = jnp.where(allowed_of(b), jnp.maximum(p - tau2 * r.grad[:, at], 0.0), 0.0)
        r.p0[:, at] = new
        r.yrow2[y, pl.ds(b, 1), :] = fold(new[WIN:])
        keep(loaded(2.0 * new - p, b), b)

    rows2_y = spread(r.yrow2, y, y_peers, r.s_rowy.at[1, 0], r.s_rowy.at[1, 1])

    store = pltpu.make_async_copy(r.sd_v, out_p, r.s_out.at[0])

    def rows_second(m):
        if m == 3:
            rows2_y()
            r.xrow2[x] = added(r.yrow2)
            rows_second.wait = spread(r.xrow2, x, x_peers, r.s_rowx.at[1, 0], r.s_rowx.at[1, 1])
        if m == 5:
            rows_second.wait()
            new = added(r.xrow2)
            out_a[...] = r.a1[...] + sigma2 * (root - (2.0 * new - r.tot1[...]) * (1.0 / root))

        if m == 3:

            @pl.loop(0, blocks)
            def _(b):
                r.sd_v[lanes_of(b), :] = r.p0[own, lanes_of(b)].T

            store.start()

    def finish_second(side, q, at, value):
        r.c2[at, :] = jnp.maximum(r.ag[z, c, at, :] + sigma2 * (value - r.capac_s[at, :]), 0.0)

    reduced_loads(1, rows_second, finish_second)
    out_c[...] = r.c2[...].T
    drain()
    store.wait()


def move(*refs):
    n = len(refs) // 2
    sems = refs[-1]
    copies = [pltpu.make_async_copy(refs[k], refs[n + k], sems.at[k]) for k in range(n)]
    for copy in copies:
        copy.start()
    for copy in copies:
        copy.wait()


def shards(sizes, all_slots, start, assign, cap, tool, dur, rel, slack, capac, jw, eta, omega):
    ny, nx = sizes
    rows, slots = start.shape
    tools = cap.shape[0]
    share = tools // (RING * CORES)
    blocks = rows // LANES
    scratch = scratch_of(rows, slots, tools, share, blocks, ny, nx)
    hbm = pl.BlockSpec(memory_space=pltpu.HBM)
    vec = pl.BlockSpec(memory_space=pltpu.VMEM)

    def tiles(v):
        return v.reshape(blocks, LANES)

    results = (
        jax.ShapeDtypeStruct((rows, slots), F32),
        jax.ShapeDtypeStruct((blocks, LANES), F32),
        jax.ShapeDtypeStruct((share, slots), F32),
    )
    found = pl.pallas_call(
        functools.partial(kernel, tuple(scratch), ny, nx, all_slots),
        out_shape=results,
        in_specs=[hbm] * 11,
        out_specs=(hbm, vec, vec),
        scratch_shapes=list(scratch.values()),
        compiler_params=pltpu.CompilerParams(
            collective_id=0, has_side_effects=True, vmem_limit_bytes=58 * 1024 * 1024
        ),
        cost_estimate=pl.CostEstimate(flops=8_600_000_000, bytes_accessed=6_000_000, transcendentals=0),
        name="pdhg",
    )(start, cap, capac, *map(tiles, (tool, dur, rel, slack, jw, assign)), eta, omega)
    p, a, c = pl.pallas_call(
        move,
        out_shape=results,
        in_specs=[vec] * 3,
        out_specs=(hbm, hbm, hbm),
        scratch_shapes=[pltpu.SemaphoreType.DMA((3,))],
        name="move",
    )(*found)
    return p, a.reshape(rows), c


def solution(mesh):
    ntm = mesh.shape["tm"]
    ny = 4 if ntm >= 16 else ntm

    def run(start, *rest):
        body = functools.partial(shards, (ny, ntm // ny), start.shape[1])
        return jax.shard_map(
            body,
            mesh=mesh,
            in_specs=(
                P("jobs", "tm"), P("jobs"), P(None, "tm"), P("jobs"), P("jobs"), P("jobs"),
                P("jobs"), P(None, "tm"), P("jobs"), P(), P(),
            ),
            out_specs=(P("jobs", "tm"), P("jobs"), P("jobs", "tm")),
            check_vma=False,
        )(start, *rest)

    return run
```

```python
import functools
import math
import types

import jax
import jax.numpy as jnp
from jax import lax
from jax.experimental import pallas as pl
from jax.experimental.pallas import tpu as pltpu
from jax.sharding import PartitionSpec as P

WIN = 32
LANES = 128
RING = 8
CORES = 2
F32, BF16 = jnp.float32, jnp.bfloat16
ORDER = (4, 3, 5, 2, 6, 1, 7, 0)
MESSAGES = 7
PIECES = 2
STRIPS = 4


def window(x, dur, backward):
    n = x.shape[0]

    def move(v, k):
        return pltpu.roll(v, k if backward else n - k, 0)

    d = jnp.broadcast_to(dur, x.shape)
    span, total = 1, x
    acc = jnp.where((d & 1) != 0, x, 0.0)
    while span < WIN // 2:
        total = total + move(total, span)
        span *= 2
        acc = jnp.where((d & span) != 0, total + move(acc, span), acc)
    total = total + move(total, span)
    return jnp.where(d == WIN, total, acc)


def summed(x, dur, backward):
    half = (x.shape[0] - WIN) // 2
    parts = (x[: half + WIN], x[half:])
    kept = slice(WIN, None) if backward else slice(0, half)
    return jnp.concatenate([window(part, dur, backward)[kept] for part in parts], axis=0)


def split(x):
    high = x.astype(BF16)
    return high, (x - high.astype(F32)).astype(BF16)


def dot(a, b, contract_b=0):
    return lax.dot_general(
        a, b, (((1,), (contract_b,)), ((), ())), preferred_element_type=F32
    )


def fold(x):
    return jnp.sum(x, axis=0, keepdims=True)


def scratch_of(rows, slots, tools, share, blocks, ny, nx):
    piece = slots // (2 * PIECES)
    dma, vmem = pltpu.SemaphoreType.DMA, pltpu.VMEM
    return dict(
        ints=vmem((4, blocks, LANES), jnp.int32),
        floats=vmem((2, blocks, LANES), F32),
        eta=pltpu.SMEM((1,), F32),
        omega=pltpu.SMEM((1,), F32),
        sd_v=vmem((rows, slots), F32),
        cap_v=vmem((tools, slots), F32),
        capac_v=vmem((share, slots), jnp.int32),
        cap_hi=vmem((tools, slots), BF16),
        cap_lo=vmem((tools, slots), BF16),
        mem=vmem((rows, tools), BF16),
        pj0=vmem((slots + 2 * WIN, rows), F32),
        pj1=vmem((slots + 2 * WIN, rows), F32),
        p0=vmem((slots + WIN, rows), F32),
        p1=vmem((slots + WIN, rows), F32),
        grad=vmem((slots + WIN, rows), F32),
        wdp=vmem((slots, rows), F32),
        ws=vmem((2 * slots, rows), BF16),
        part=vmem((RING, CORES, slots, share), F32),
        pairbuf=vmem((2, RING, slots, share), F32),
        rsu=vmem((2, MESSAGES, PIECES, piece, share), F32),
        rsd=vmem((2, MESSAGES, PIECES, piece, share), F32),
        ag=vmem((RING, CORES, slots, share), F32),
        cap_s=vmem((slots, share), F32),
        capac_s=vmem((slots, share), F32),
        c2=vmem((slots, share), F32),
        yrow=vmem((ny, 2 * blocks, LANES), F32),
        xrow=vmem((nx, 2 * blocks, LANES), F32),
        yrow2=vmem((ny, blocks, LANES), F32),
        xrow2=vmem((nx, blocks, LANES), F32),
        tot1=vmem((blocks, LANES), F32),
        a1=vmem((blocks, LANES), F32),
        accp=vmem((8, LANES), F32),
        sc_j=vmem((RING * CORES, 8, LANES), F32),
        sc_t=vmem((ny * nx, 8, LANES), F32),
        s_load=dma((11,)),
        s_out=dma((1,)),
        s_halo=dma((2, 5)),
        s_up=dma((2, 3, MESSAGES, PIECES)),
        s_dn=dma((2, 3, MESSAGES, PIECES)),
        s_pair=dma((2, 2, RING)),
        s_sib=dma((2, 2 * RING)),
        s_rowy=dma((2, 2, ny)),
        s_rowx=dma((2, 2, nx)),
        s_scj=dma((2, RING * CORES)),
        s_sct=dma((2, ny * nx)),
    )


def kernel(
    names, ny, nx, all_slots, sd, cap, capac, tool_in, dur_in, rel_in, slack_in, jw_in, assign_in,
    eta_in, omega_in, out_p, out_a, out_c, *scratch,
):
    r = types.SimpleNamespace(**dict(zip(names, scratch)))
    rows, slots = r.sd_v.shape
    tools, share = r.cap_v.shape[0], r.capac_v.shape[0]
    blocks, half, ntm = rows // LANES, slots // 2, ny * nx
    piece = half // PIECES
    pair = CORES * share
    root = math.sqrt(all_slots)

    mj, mt = lax.axis_index("jobs"), lax.axis_index("tm")
    z, c = lax.div(mj, CORES), lax.rem(mj, CORES)
    x, y = lax.div(mt, ny), lax.rem(mt, ny)

    def zline(k):
        return lax.rem(z + k, RING) * CORES + c

    sibling = (z * CORES + 1 - c, mt)
    above, below = (zline(1), mt), (zline(RING - 1), mt)
    after, before = (mj, lax.rem(mt + 1, ntm)), (mj, lax.rem(mt + ntm - 1, ntm))
    far = sorted(range(1, RING * CORES), key=lambda k: -min(k, RING * CORES - k))
    j_peers = [(lax.rem(mj + k, RING * CORES), (lax.rem(mj + k, RING * CORES), mt)) for k in far]
    y_peers = [(lax.rem(y + k, ny), (mj, x * ny + lax.rem(y + k, ny))) for k in range(1, ny)]
    x_peers = [(lax.rem(x + k, nx), (mj, lax.rem(x + k, nx) * ny + y)) for k in range(1, nx)]

    t_peers = [(lax.rem(mt + k, ntm), (mj, lax.rem(mt + k, ntm))) for k in range(1, ntm)]
    tool, dur, rel, slack = (r.ints.at[k] for k in range(4))
    jw, assign = (r.floats.at[k] for k in range(2))

    sent = []

    def remote(src, dst, ssem, rsem, device):
        return pltpu.make_async_remote_copy(
            src_ref=src, dst_ref=dst, send_sem=ssem, recv_sem=rsem,
            device_id=device, device_id_type=pl.DeviceIdType.MESH,
        )

    def send(*args):
        copy = remote(*args)
        copy.start()
        sent.append(copy)

    def arrived(dst, ssem, rsem, device):
        remote(dst, dst, ssem, rsem, device).wait_recv()

    def drain():
        for copy in sent:
            copy.wait_send()
        sent.clear()

    def spread(buf, mine, peers, ssem, rsem):
        for k, (_, device) in enumerate(peers):
            send(buf.at[mine], buf.at[mine], ssem.at[k], rsem.at[mine], device)

        def wait():
            for k, (index, device) in enumerate(peers):
                arrived(buf.at[index], ssem.at[k], rsem.at[index], device)

        return wait

    def added(buf):
        total = buf[0]
        for k in range(1, buf.shape[0]):
            total = total + buf[k]
        return total

    barrier = pltpu.get_barrier_semaphore()
    partners = [sibling, above, below, before, after]
    partners += [device for group in (y_peers, x_peers) for _, device in group]
    for device in partners:
        pl.semaphore_signal(barrier, inc=1, device_id=device, device_id_type=pl.DeviceIdType.MESH)
    first_tool = pl.multiple_of(mj * share, share)
    loads = [
        pltpu.make_async_copy(source, target, r.s_load.at[k])
        for k, (source, target) in enumerate(
            [
                (tool_in, tool), (cap, r.cap_v), (sd, r.sd_v), (dur_in, dur), (rel_in, rel), (slack_in, slack),
                (jw_in, jw), (assign_in, assign), (eta_in, r.eta), (omega_in, r.omega),
                (capac.at[pl.ds(first_tool, share), :], r.capac_v),
            ]
        )
    ]
    for copy in loads:
        copy.start()
    loads[0].wait()

    lane = lax.broadcasted_iota(jnp.int32, (LANES, LANES), 1).astype(F32)

    @pl.loop(0, blocks)
    def _(b):
        row = jnp.broadcast_to(tool[pl.ds(b, 1), :].astype(F32), (LANES, LANES))
        column = row.T
        for k in range(tools // LANES):
            hit = jnp.where(column == lane + float(k * LANES), 1.0, 0.0).astype(BF16)
            r.mem[pl.ds(pl.multiple_of(b * LANES, LANES), LANES), k * LANES : (k + 1) * LANES] = hit

    loads[1].wait()

    @pl.loop(0, tools // share)
    def _(b):
        at = pl.ds(pl.multiple_of(b * share, share), share)
        high, low = split(r.cap_v[at, :])
        r.cap_hi[at, :] = high
        r.cap_lo[at, :] = low

    step = min(rows, 256)

    @pl.loop(0, rows // step)
    def _(b):
        at = pl.ds(pl.multiple_of(b * step, step), step)
        m = r.mem[at, :]
        found = dot(m, r.cap_hi[...]) + dot(m, r.cap_lo[...])
        r.pj0[WIN : WIN + slots, at] = found.T

    def lanes_of(b):
        return pl.ds(pl.multiple_of(b * LANES, LANES), LANES)

    slot = lax.broadcasted_iota(jnp.int32, (slots + WIN, LANES), 0) + (mt * slots - WIN)
    own = slice(WIN, WIN + slots)

    def allowed_of(b, s=slot):
        return (s >= rel[pl.ds(b, 1), :]) & (s + dur[pl.ds(b, 1), :] <= all_slots)

    def cost_of(b, s=slot):
        d = dur[pl.ds(b, 1), :]
        due = rel[pl.ds(b, 1), :] + d + slack[pl.ds(b, 1), :]
        end = s + d
        late = jnp.maximum(end - due, 0)
        return jw[pl.ds(b, 1), :] * (
            end.astype(F32) * (1.0 / all_slots) + late.astype(F32) * (1.0 / (4 * WIN))
        )

    for copy in loads[2:]:
        copy.wait()
    weight, eta = r.omega[0], r.eta[0]
    tau1, sigma1 = eta / weight, eta * weight

    @pl.loop(0, blocks)
    def _(b):
        start = r.sd_v[lanes_of(b), :].T
        p = jnp.where(allowed_of(b, slot[WIN:]), start, 0.0)
        r.p0[own, lanes_of(b)] = p
        r.yrow[y, pl.ds(blocks + b, 1), :] = fold(p)

    pl.semaphore_wait(barrier, len(partners))

    def halo(k, src, dst, device):
        send(src, dst, r.s_halo.at[0, k], r.s_halo.at[1, k], device)

    def halo_arrived(k, dst, device):
        arrived(dst, r.s_halo.at[0, k], r.s_halo.at[1, k], device)

    lead, head = pl.ds(0, WIN), pl.ds(WIN, WIN)
    tail, beyond = pl.ds(slots, WIN), pl.ds(slots + WIN, WIN)

    def exchange(k, buf):
        halo(k, buf.at[head, :], buf.at[beyond, :], before)
        halo(k + 1, buf.at[tail, :], buf.at[lead, :], after)

        def wait():
            halo_arrived(k, buf.at[beyond, :], after)
            halo_arrived(k + 1, buf.at[lead, :], before)

        return wait

    duals_wait = exchange(0, r.pj0)
    halo(2, r.p0.at[tail, :], r.p0.at[lead, :], after)

    r.cap_s[...] = r.cap_v[pl.ds(first_tool, share), :].T
    r.capac_s[...] = r.capac_v[...].astype(F32).T

    def adjoint(buf, b):
        at = lanes_of(b)
        past = jnp.where(mt == ntm - 1, 0.0, buf[beyond, at])
        x = jnp.concatenate([buf[0 : slots + WIN, at], past], axis=0)
        return summed(x, dur[pl.ds(b, 1), :], False) * (1.0 / WIN)

    def loaded(x, b):
        return summed(x, dur[pl.ds(b, 1), :], True)

    def keep(w, b, first=0):
        high, low = split(w)
        n = w.shape[0]
        r.ws[first : first + n, lanes_of(b)] = high
        r.ws[slots + first : slots + first + n, lanes_of(b)] = low

    inner = slice(WIN, slots)
    r.accp[...] = jnp.zeros_like(r.accp)

    def updated(b, s, p, adj):
        gradient = cost_of(b, s) - assign[pl.ds(b, 1), :] * (1.0 / root) + adj * (1.0 / WIN)
        return jnp.where(allowed_of(b, s), jnp.maximum(p - tau1 * gradient, 0.0), 0.0)

    @pl.loop(0, blocks)
    def _(b):
        at = lanes_of(b)
        p = r.p0[inner, at]
        adj = summed(r.pj0[own, at], dur[pl.ds(b, 1), :], False)
        new = updated(b, slot[inner], p, adj)
        r.p1[inner, at] = new
        r.yrow[y, pl.ds(b, 1), :] = fold(new)
        moved = new - p
        r.accp[0:1, :] += fold(moved * moved)
        w = loaded(2.0 * new - p, b)
        r.wdp[WIN : slots - WIN, at] = 0.5 * (w - loaded(p, b))
        keep(w, b, WIN)

    duals_wait()
    halo_arrived(2, r.p0.at[lead, :], before)
    low, high = slice(0, WIN), slice(2 * WIN, 3 * WIN)
    edges = jnp.concatenate([slot[:WIN], slot[slots:]], axis=0)

    @pl.loop(0, blocks)
    def _(b):
        at = lanes_of(b)
        past = jnp.where(mt == ntm - 1, 0.0, r.pj0[beyond, at])
        bands = jnp.concatenate([r.pj0[: 2 * WIN, at], r.pj0[tail, at], past], axis=0)
        adj = window(bands, dur[pl.ds(b, 1), :], False)
        adj = jnp.concatenate([adj[low], adj[high]], axis=0)
        p = jnp.concatenate([r.p0[lead, at], r.p0[tail, at]], axis=0)
        p = jnp.where(allowed_of(b, edges), p, 0.0)
        new = updated(b, edges, p, adj)
        r.p1[lead, at] = new[:WIN]
        r.p1[tail, at] = new[WIN:]
        r.yrow[y, pl.ds(b, 1), :] += fold(new[WIN:])
        moved = (new - p)[WIN:]
        r.accp[0:1, :] += fold(moved * moved)
        inside = pl.ds(slots - WIN, WIN)
        old = jnp.concatenate([p[:WIN], r.p0[head, at], r.p0[inside, at], p[WIN:]], axis=0)
        now = jnp.concatenate([new[:WIN], r.p1[head, at], r.p1[inside, at], new[WIN:]], axis=0)
        w, v = (window(x, dur[pl.ds(b, 1), :], True) for x in (2.0 * now - old, old))
        for first, k in ((0, WIN), (slots - WIN, 3 * WIN)):
            r.wdp[first : first + WIN, at] = 0.5 * (w[k : k + WIN] - v[k : k + WIN])
            keep(w[k : k + WIN], b, first)

    rows_y = spread(r.yrow, y, y_peers, r.s_rowy.at[0, 0], r.s_rowy.at[0, 1])

    def rows_of(side, q):
        return pl.ds(side * half + q * piece, piece)

    def reduced_loads(it, extra, finish):
        paired = set()

        def produce(i):
            owner = lax.rem(z + ORDER[i], RING)
            full = dot(r.ws[...], r.mem[:, pl.ds(pl.multiple_of(owner * pair, pair), pair)])
            full = (full[:slots] + full[slots:]) * (1.0 / WIN)
            r.part[i, 0] = full[:, :share]
            r.part[i, 1] = full[:, share:]
            send(r.part.at[i, 1 - c], r.pairbuf.at[it, i], r.s_pair.at[it, 0, i], r.s_pair.at[it, 1, i], sibling)

        def mine(i, side, q):
            if i not in paired:
                arrived(r.pairbuf.at[it, i], r.s_pair.at[it, 0, i], r.s_pair.at[it, 1, i], sibling)
                paired.add(i)
            at = rows_of(side, q)
            return r.part[i, c, at, :] + r.pairbuf[it, i, at, :]

        def incoming(upward, m, q):
            buf, sems, source = (r.rsu, r.s_up, below) if upward else (r.rsd, r.s_dn, above)
            arrived(buf.at[it, m, q], sems.at[it, 0, m, q], sems.at[it, 1, m, q], source)
            return buf[it, m, q]

        def message(m, q, upward):
            buf, sems, to = (r.rsu, r.s_up, above) if upward else (r.rsd, r.s_dn, below)
            distance = 4 - (m + 1) // 2
            i = ORDER.index(distance if upward else RING - distance)
            side = m % 2 if upward else 1 - m % 2
            value = mine(i, side, q)
            if m >= 2:
                value = value + incoming(upward, m - 2, q)
            at = rows_of(side, q)
            r.part[i, c, at, :] = value
            send(r.part.at[i, c, at, :], buf.at[it, m, q], sems.at[it, 0, m, q], sems.at[it, 1, m, q], to)

        ready = {0: 3, 1: 3, 2: 5, 3: 5, 4: 7, 5: 7}
        done = 0
        for m in range(MESSAGES):
            while done < ready.get(m, RING):
                produce(done)
                done += 1
            for q in range(PIECES):
                message(m, q, True)
                message(m, q, False)
            extra(m)
        i = ORDER.index(0)
        for q in range(PIECES):
            for side in (0, 1):
                value = mine(i, side, q) + incoming(True, 6 - side, q) + incoming(False, 5 + side, q)
                finish(side, q, rows_of(side, q), value)

    def rows_first(m):
        if m == 3:
            rows_y()
            r.xrow[x] = added(r.yrow)
            rows_first.wait = spread(r.xrow, x, x_peers, r.s_rowx.at[0, 0], r.s_rowx.at[0, 1])
        if m == MESSAGES + 1:
            rows_first.wait()
            total = added(r.xrow)
            new, old = total[:blocks], total[blocks:]
            r.tot1[...] = new
            delta = sigma1 * (root - (2.0 * new - old) * (1.0 / root))
            r.a1[...] = assign[...] + delta
            once = jnp.where(mt == 0, 1.0, 0.0)
            r.accp[3:4, :] = once * fold(delta * delta)
            r.accp[4:5, :] = once * fold(delta * (new - old))

    def part_of(hops, side, q=None):
        at = pl.ds(side * half, half) if q is None else rows_of(side, q)
        return (lax.rem(z + hops + RING, RING), c, at, slice(None))

    def pass_on(m, q, upward):
        sems, to = (r.s_up, above) if upward else (r.s_dn, below)
        hops = -(m // 2) if upward else m // 2
        at = part_of(hops, m % 2 if upward else 1 - m % 2, q)
        send(r.ag.at[at], r.ag.at[at], sems.at[0, 2, m, q], sems.at[1, 2, m, q], to)

    def across(hops, side):
        k = 2 * (hops % RING) + side
        at = part_of(hops, side)
        send(r.ag.at[at], r.ag.at[at], r.s_sib.at[0, k], r.s_sib.at[1, k], sibling)

    def finish_first(side, q, at, value):
        old = r.cap_s[at, :]
        new = jnp.maximum(old + sigma1 * (value - r.capac_s[at, :]), 0.0)
        r.ag[z, c, at, :] = new
        pass_on(side, q, True)
        pass_on(1 - side, q, False)
        moved = new - old
        r.accp[1:2, :] += fold(moved * moved)
        if q == PIECES - 1:
            across(0, side)

    reduced_loads(0, rows_first, finish_first)

    def crossed(hops, side):
        k = 2 * (hops % RING) + side
        at = (lax.rem(z + hops + RING, RING), 1 - c, pl.ds(side * half, half), slice(None))
        arrived(r.ag.at[at], r.s_sib.at[0, k], r.s_sib.at[1, k], sibling)

    def gather(hops, first=False):
        crossed(hops, 0)
        crossed(hops, 1)
        owner = lax.rem(z + hops + RING, RING)
        high, low = split(jnp.concatenate([r.ag[owner, 0], r.ag[owner, 1]], axis=1))
        both = jnp.concatenate([high, low], axis=0)
        full = dot(both, r.mem[:, pl.ds(pl.multiple_of(owner * pair, pair), pair)], 1)
        full = full[:slots] + full[slots:]
        r.pj1[own, :] = full if first else r.pj1[own, :] + full

    work = {1: (0,), 3: (-1, 1), 5: (-2, 2), 6: (-3, 3)}
    for m in range(MESSAGES):
        for upward in (True, False):
            hops = -1 - m // 2 if upward else 1 + m // 2
            side = m % 2 if upward else 1 - m % 2
            sems, source = (r.s_up, below) if upward else (r.s_dn, above)
            for q in range(PIECES):
                arrived(r.ag.at[part_of(hops, side, q)], sems.at[0, 2, m, q], sems.at[1, 2, m, q], source)
                if m + 2 < MESSAGES:
                    pass_on(m + 2, q, upward)
            across(hops, side)
        for hops in work.get(m, ()):
            gather(hops, first=hops == 0)
        rows_first(MESSAGES + m)
    gather(4)

    duals_wait = exchange(3, r.pj1)

    @pl.loop(0, blocks)
    def _(b):
        at = lanes_of(b)
        r.accp[2:3, :] += fold((r.pj1[own, at] - r.pj0[own, at]) * r.wdp[:, at]) * (1.0 / WIN)

    r.sc_j[mj] = r.accp[...]
    spread(r.sc_j, mj, j_peers, r.s_scj.at[0], r.s_scj.at[1])()
    r.sc_t[mt] = added(r.sc_j)
    sums_wait = spread(r.sc_t, mt, t_peers, r.s_sct.at[0], r.s_sct.at[1])
    duals_wait()

    @pl.loop(0, blocks)
    def _(b):
        r.grad[:, lanes_of(b)] = cost_of(b) - r.a1[pl.ds(b, 1), :] * (1.0 / root) + adjoint(r.pj1, b)

    sums_wait()
    sums = jnp.sum(added(r.sc_t), axis=1, keepdims=True)
    sum_primal, sum_cap, cross_primal, sum_assign, cross_assign = (sums[k : k + 1] for k in range(5))
    movement = weight * 0.5 * sum_primal + (sum_assign + sum_cap) / (2.0 * weight)
    interaction = jnp.abs(cross_primal - cross_assign * (1.0 / root))
    step_next = movement / (interaction + movement / (1.5 * eta))
    tau2 = jnp.broadcast_to(step_next / weight, (1, LANES))
    sigma2 = jnp.broadcast_to(step_next * weight, (1, LANES))

    drain()

    @pl.loop(0, blocks)
    def _(b):
        at = lanes_of(b)
        p = r.p1[:, at]
        new = jnp.where(allowed_of(b), jnp.maximum(p - tau2 * r.grad[:, at], 0.0), 0.0)
        r.p0[:, at] = new
        r.yrow2[y, pl.ds(b, 1), :] = fold(new[WIN:])
        keep(loaded(2.0 * new - p, b), b)

    rows2_y = spread(r.yrow2, y, y_peers, r.s_rowy.at[1, 0], r.s_rowy.at[1, 1])

    store = pltpu.make_async_copy(r.sd_v, out_p, r.s_out.at[0])

    def rows_second(m):
        if m == 3:
            rows2_y()
            r.xrow2[x] = added(r.yrow2)
            rows_second.wait = spread(r.xrow2, x, x_peers, r.s_rowx.at[1, 0], r.s_rowx.at[1, 1])
        if m == 5:
            rows_second.wait()
            new = added(r.xrow2)
            out_a[...] = r.a1[...] + sigma2 * (root - (2.0 * new - r.tot1[...]) * (1.0 / root))

        if m == 3:

            @pl.loop(0, blocks)
            def _(b):
                r.sd_v[lanes_of(b), :] = r.p0[own, lanes_of(b)].T

            store.start()

    def finish_second(side, q, at, value):
        r.c2[at, :] = jnp.maximum(r.ag[z, c, at, :] + sigma2 * (value - r.capac_s[at, :]), 0.0)

    reduced_loads(1, rows_second, finish_second)
    out_c[...] = r.c2[...].T
    drain()
    store.wait()


def move(p, a, c, p_out, a_out, c_out, p_v, a_v, c_v, sem_in, sem_out):
    rows = p.shape[0] // STRIPS
    ways = [(a, a_v, a_out), (c, c_v, c_out)]
    for k in range(STRIPS):
        at = pl.ds(k * rows, rows)
        ways.append((p.at[at, :], p_v.at[at, :], p_out.at[at, :]))
    copies_in = [pltpu.make_async_copy(w[0], w[1], sem_in.at[k]) for k, w in enumerate(ways)]
    copies_out = [pltpu.make_async_copy(w[1], w[2], sem_out.at[k]) for k, w in enumerate(ways)]
    for copy in copies_in:
        copy.start()
    for before, after in zip(copies_in, copies_out):
        before.wait()
        after.start()
    for copy in copies_out:
        copy.wait()


def shards(sizes, all_slots, start, assign, cap, tool, dur, rel, slack, capac, jw, eta, omega):
    ny, nx = sizes
    rows, slots = start.shape
    tools = cap.shape[0]
    share = tools // (RING * CORES)
    blocks = rows // LANES
    scratch = scratch_of(rows, slots, tools, share, blocks, ny, nx)
    hbm = pl.BlockSpec(memory_space=pltpu.HBM)
    vec = pl.BlockSpec(memory_space=pltpu.VMEM)

    def tiles(v):
        return v.reshape(blocks, LANES)

    results = (
        jax.ShapeDtypeStruct((rows, slots), F32),
        jax.ShapeDtypeStruct((blocks, LANES), F32),
        jax.ShapeDtypeStruct((share, slots), F32),
    )
    found = pl.pallas_call(
        functools.partial(kernel, tuple(scratch), ny, nx, all_slots),
        out_shape=results,
        in_specs=[hbm] * 11,
        out_specs=(hbm, vec, vec),
        scratch_shapes=list(scratch.values()),
        compiler_params=pltpu.CompilerParams(
            collective_id=0, has_side_effects=True, vmem_limit_bytes=58 * 1024 * 1024
        ),
        cost_estimate=pl.CostEstimate(flops=8_600_000_000, bytes_accessed=6_000_000, transcendentals=0),
        name="pdhg",
    )(start, cap, capac, *map(tiles, (tool, dur, rel, slack, jw, assign)), eta, omega)
    p, a, c = pl.pallas_call(
        move,
        out_shape=results,
        in_specs=[hbm] * 3,
        out_specs=(hbm, hbm, hbm),
        scratch_shapes=[pltpu.VMEM(result.shape, F32) for result in results]
        + [pltpu.SemaphoreType.DMA((2 + STRIPS,))] * 2,
        name="move",
    )(*found)
    return p, a.reshape(rows), c


def solution(mesh):
    ntm = mesh.shape["tm"]
    ny = 4 if ntm >= 16 else ntm

    def run(start, *rest):
        body = functools.partial(shards, (ny, ntm // ny), start.shape[1])
        return jax.shard_map(
            body,
            mesh=mesh,
            in_specs=(
                P("jobs", "tm"), P("jobs"), P(None, "tm"), P("jobs"), P("jobs"), P("jobs"),
                P("jobs"), P(None, "tm"), P("jobs"), P(), P(),
            ),
            out_specs=(P("jobs", "tm"), P("jobs"), P("jobs", "tm")),
            check_vma=False,
        )(start, *rest)

    return run
```

```python
import functools
import math
import types

import jax
import jax.numpy as jnp
from jax import lax
from jax.experimental import pallas as pl
from jax.experimental.pallas import tpu as pltpu
from jax.sharding import PartitionSpec as P

WIN = 32
LANES = 128
RING = 8
CORES = 2
F32, BF16 = jnp.float32, jnp.bfloat16
ORDER = (4, 3, 5, 2, 6, 1, 7, 0)
MESSAGES = 7
PIECES = 2
STRIPS = 4


def window(x, dur, backward):
    n = x.shape[0]

    def move(v, k):
        return pltpu.roll(v, k if backward else n - k, 0)

    d = jnp.broadcast_to(dur, x.shape)
    span, total = 1, x
    acc = jnp.where((d & 1) != 0, x, 0.0)
    while span < WIN // 2:
        total = total + move(total, span)
        span *= 2
        acc = jnp.where((d & span) != 0, total + move(acc, span), acc)
    total = total + move(total, span)
    return jnp.where(d == WIN, total, acc)


def summed(x, dur, backward):
    half = (x.shape[0] - WIN) // 2
    parts = (x[: half + WIN], x[half:])
    kept = slice(WIN, None) if backward else slice(0, half)
    return jnp.concatenate([window(part, dur, backward)[kept] for part in parts], axis=0)


def split(x):
    high = x.astype(BF16)
    return high, (x - high.astype(F32)).astype(BF16)


def dot(a, b, contract_b=0):
    return lax.dot_general(
        a, b, (((1,), (contract_b,)), ((), ())), preferred_element_type=F32
    )


def fold(x):
    return jnp.sum(x, axis=0, keepdims=True)


def scratch_of(rows, slots, tools, share, blocks, ny, nx):
    piece = slots // (2 * PIECES)
    dma, vmem = pltpu.SemaphoreType.DMA, pltpu.VMEM
    return dict(
        ints=vmem((4, blocks, LANES), jnp.int32),
        floats=vmem((2, blocks, LANES), F32),
        eta=pltpu.SMEM((1,), F32),
        omega=pltpu.SMEM((1,), F32),
        sd_v=vmem((rows, slots), F32),
        cap_v=vmem((tools, slots), F32),
        capac_v=vmem((share, slots), jnp.int32),
        cap_hi=vmem((tools, slots), BF16),
        cap_lo=vmem((tools, slots), BF16),
        mem=vmem((rows, tools), BF16),
        pj0=vmem((slots + 2 * WIN, rows), F32),
        pj1=vmem((slots + 2 * WIN, rows), F32),
        p0=vmem((slots + WIN, rows), F32),
        p1=vmem((slots + WIN, rows), F32),
        grad=vmem((slots + WIN, rows), F32),
        wdp=vmem((slots, rows), F32),
        ws=vmem((2 * slots, rows), BF16),
        part=vmem((RING, CORES, slots, share), F32),
        pairbuf=vmem((2, RING, slots, share), F32),
        rsu=vmem((2, MESSAGES, PIECES, piece, share), F32),
        rsd=vmem((2, MESSAGES, PIECES, piece, share), F32),
        ag=vmem((RING, CORES, slots, share), F32),
        cap_s=vmem((slots, share), F32),
        capac_s=vmem((slots, share), F32),
        c2=vmem((slots, share), F32),
        yrow=vmem((ny, 2 * blocks, LANES), F32),
        xrow=vmem((nx, 2 * blocks, LANES), F32),
        yrow2=vmem((ny, blocks, LANES), F32),
        xrow2=vmem((nx, blocks, LANES), F32),
        tot1=vmem((blocks, LANES), F32),
        a1=vmem((blocks, LANES), F32),
        accp=vmem((8, LANES), F32),
        sc_j=vmem((RING * CORES, 8, LANES), F32),
        sc_t=vmem((ny * nx, 8, LANES), F32),
        s_load=dma((11,)),
        s_out=dma((1,)),
        s_halo=dma((2, 5)),
        s_up=dma((2, 3, MESSAGES, PIECES)),
        s_dn=dma((2, 3, MESSAGES, PIECES)),
        s_pair=dma((2, 2, RING)),
        s_sib=dma((2, 2 * RING)),
        s_rowy=dma((2, 2, ny)),
        s_rowx=dma((2, 2, nx)),
        s_scj=dma((2, RING * CORES)),
        s_sct=dma((2, ny * nx)),
    )


def kernel(
    names, ny, nx, all_slots, sd, cap, capac, tool_in, dur_in, rel_in, slack_in, jw_in, assign_in,
    eta_in, omega_in, out_p, out_a, out_c, *scratch,
):
    r = types.SimpleNamespace(**dict(zip(names, scratch)))
    rows, slots = r.sd_v.shape
    tools, share = r.cap_v.shape[0], r.capac_v.shape[0]
    blocks, half, ntm = rows // LANES, slots // 2, ny * nx
    piece = half // PIECES
    pair = CORES * share
    root = math.sqrt(all_slots)

    mj, mt = lax.axis_index("jobs"), lax.axis_index("tm")
    z, c = lax.div(mj, CORES), lax.rem(mj, CORES)
    x, y = lax.div(mt, ny), lax.rem(mt, ny)

    def zline(k):
        return lax.rem(z + k, RING) * CORES + c

    sibling = (z * CORES + 1 - c, mt)
    above, below = (zline(1), mt), (zline(RING - 1), mt)
    after, before = (mj, lax.rem(mt + 1, ntm)), (mj, lax.rem(mt + ntm - 1, ntm))
    far = sorted(range(1, RING * CORES), key=lambda k: -min(k, RING * CORES - k))
    j_peers = [(lax.rem(mj + k, RING * CORES), (lax.rem(mj + k, RING * CORES), mt)) for k in far]
    y_peers = [(lax.rem(y + k, ny), (mj, x * ny + lax.rem(y + k, ny))) for k in range(1, ny)]
    x_peers = [(lax.rem(x + k, nx), (mj, lax.rem(x + k, nx) * ny + y)) for k in range(1, nx)]

    moves = [(i, j) for i in range(nx) for j in range(ny) if i or j]
    moves.sort(key=lambda v: -min(v[0], nx - v[0]) - min(v[1], ny - v[1]))
    t_peers = [lax.rem(x + i, nx) * ny + lax.rem(y + j, ny) for i, j in moves]
    t_peers = [(k, (mj, k)) for k in t_peers]
    tool, dur, rel, slack = (r.ints.at[k] for k in range(4))
    jw, assign = (r.floats.at[k] for k in range(2))

    sent = []

    def remote(src, dst, ssem, rsem, device):
        return pltpu.make_async_remote_copy(
            src_ref=src, dst_ref=dst, send_sem=ssem, recv_sem=rsem,
            device_id=device, device_id_type=pl.DeviceIdType.MESH,
        )

    def send(*args):
        copy = remote(*args)
        copy.start()
        sent.append(copy)

    def arrived(dst, ssem, rsem, device):
        remote(dst, dst, ssem, rsem, device).wait_recv()

    def drain():
        for copy in sent:
            copy.wait_send()
        sent.clear()

    def spread(buf, mine, peers, ssem, rsem):
        for k, (_, device) in enumerate(peers):
            send(buf.at[mine], buf.at[mine], ssem.at[k], rsem.at[mine], device)

        def wait():
            for k, (index, device) in enumerate(peers):
                arrived(buf.at[index], ssem.at[k], rsem.at[index], device)

        return wait

    def added(buf):
        total = buf[0]
        for k in range(1, buf.shape[0]):
            total = total + buf[k]
        return total

    barrier = pltpu.get_barrier_semaphore()
    partners = [sibling, above, below, before, after]
    partners += [device for group in (y_peers, x_peers) for _, device in group]
    for device in partners:
        pl.semaphore_signal(barrier, inc=1, device_id=device, device_id_type=pl.DeviceIdType.MESH)
    first_tool = pl.multiple_of(mj * share, share)
    loads = [
        pltpu.make_async_copy(source, target, r.s_load.at[k])
        for k, (source, target) in enumerate(
            [
                (tool_in, tool), (cap, r.cap_v), (sd, r.sd_v), (dur_in, dur), (rel_in, rel), (slack_in, slack),
                (jw_in, jw), (assign_in, assign), (eta_in, r.eta), (omega_in, r.omega),
                (capac.at[pl.ds(first_tool, share), :], r.capac_v),
            ]
        )
    ]
    for copy in loads:
        copy.start()
    loads[0].wait()

    lane = lax.broadcasted_iota(jnp.int32, (LANES, LANES), 1).astype(F32)

    @pl.loop(0, blocks, unroll=2)
    def _(b):
        row = jnp.broadcast_to(tool[pl.ds(b, 1), :].astype(F32), (LANES, LANES))
        column = row.T
        for k in range(tools // LANES):
            hit = jnp.where(column == lane + float(k * LANES), 1.0, 0.0).astype(BF16)
            r.mem[pl.ds(pl.multiple_of(b * LANES, LANES), LANES), k * LANES : (k + 1) * LANES] = hit

    loads[1].wait()

    @pl.loop(0, tools // share)
    def _(b):
        at = pl.ds(pl.multiple_of(b * share, share), share)
        high, low = split(r.cap_v[at, :])
        r.cap_hi[at, :] = high
        r.cap_lo[at, :] = low

    step = min(rows, 256)

    @pl.loop(0, rows // step)
    def _(b):
        at = pl.ds(pl.multiple_of(b * step, step), step)
        m = r.mem[at, :]
        found = dot(m, r.cap_hi[...]) + dot(m, r.cap_lo[...])
        r.pj0[WIN : WIN + slots, at] = found.T

    def lanes_of(b):
        return pl.ds(pl.multiple_of(b * LANES, LANES), LANES)

    slot = lax.broadcasted_iota(jnp.int32, (slots + WIN, LANES), 0) + (mt * slots - WIN)
    own = slice(WIN, WIN + slots)

    def allowed_of(b, s=slot):
        return (s >= rel[pl.ds(b, 1), :]) & (s + dur[pl.ds(b, 1), :] <= all_slots)

    def cost_of(b, s=slot):
        d = dur[pl.ds(b, 1), :]
        due = rel[pl.ds(b, 1), :] + d + slack[pl.ds(b, 1), :]
        end = s + d
        late = jnp.maximum(end - due, 0)
        return jw[pl.ds(b, 1), :] * (
            end.astype(F32) * (1.0 / all_slots) + late.astype(F32) * (1.0 / (4 * WIN))
        )

    for copy in loads[2:]:
        copy.wait()
    weight, eta = r.omega[0], r.eta[0]
    tau1, sigma1 = eta / weight, eta * weight

    @pl.loop(0, blocks, unroll=2)
    def _(b):
        start = r.sd_v[lanes_of(b), :].T
        p = jnp.where(allowed_of(b, slot[WIN:]), start, 0.0)
        r.p0[own, lanes_of(b)] = p
        r.yrow[y, pl.ds(blocks + b, 1), :] = fold(p)

    pl.semaphore_wait(barrier, len(partners))

    def halo(k, src, dst, device):
        send(src, dst, r.s_halo.at[0, k], r.s_halo.at[1, k], device)

    def halo_arrived(k, dst, device):
        arrived(dst, r.s_halo.at[0, k], r.s_halo.at[1, k], device)

    lead, head = pl.ds(0, WIN), pl.ds(WIN, WIN)
    tail, beyond = pl.ds(slots, WIN), pl.ds(slots + WIN, WIN)

    def exchange(k, buf):
        halo(k, buf.at[head, :], buf.at[beyond, :], before)
        halo(k + 1, buf.at[tail, :], buf.at[lead, :], after)

        def wait():
            halo_arrived(k, buf.at[beyond, :], after)
            halo_arrived(k + 1, buf.at[lead, :], before)

        return wait

    duals_wait = exchange(0, r.pj0)
    halo(2, r.p0.at[tail, :], r.p0.at[lead, :], after)

    r.cap_s[...] = r.cap_v[pl.ds(first_tool, share), :].T
    r.capac_s[...] = r.capac_v[...].astype(F32).T

    def adjoint(buf, b):
        at = lanes_of(b)
        past = jnp.where(mt == ntm - 1, 0.0, buf[beyond, at])
        x = jnp.concatenate([buf[0 : slots + WIN, at], past], axis=0)
        return summed(x, dur[pl.ds(b, 1), :], False) * (1.0 / WIN)

    def loaded(x, b):
        return summed(x, dur[pl.ds(b, 1), :], True)

    def keep(w, b, first=0):
        high, low = split(w)
        n = w.shape[0]
        r.ws[first : first + n, lanes_of(b)] = high
        r.ws[slots + first : slots + first + n, lanes_of(b)] = low

    inner = slice(WIN, slots)
    r.accp[...] = jnp.zeros_like(r.accp)

    def updated(b, s, p, adj):
        gradient = cost_of(b, s) - assign[pl.ds(b, 1), :] * (1.0 / root) + adj * (1.0 / WIN)
        return jnp.where(allowed_of(b, s), jnp.maximum(p - tau1 * gradient, 0.0), 0.0)

    @pl.loop(0, blocks, unroll=2)
    def _(b):
        at = lanes_of(b)
        p = r.p0[inner, at]
        adj = summed(r.pj0[own, at], dur[pl.ds(b, 1), :], False)
        new = updated(b, slot[inner], p, adj)
        r.p1[inner, at] = new
        r.yrow[y, pl.ds(b, 1), :] = fold(new)
        moved = new - p
        r.accp[0:1, :] += fold(moved * moved)
        w = loaded(2.0 * new - p, b)
        r.wdp[WIN : slots - WIN, at] = 0.5 * (w - loaded(p, b))
        keep(w, b, WIN)

    duals_wait()
    halo_arrived(2, r.p0.at[lead, :], before)
    low, high = slice(0, WIN), slice(2 * WIN, 3 * WIN)
    edges = jnp.concatenate([slot[:WIN], slot[slots:]], axis=0)

    @pl.loop(0, blocks, unroll=2)
    def _(b):
        at = lanes_of(b)
        past = jnp.where(mt == ntm - 1, 0.0, r.pj0[beyond, at])
        bands = jnp.concatenate([r.pj0[: 2 * WIN, at], r.pj0[tail, at], past], axis=0)
        adj = window(bands, dur[pl.ds(b, 1), :], False)
        adj = jnp.concatenate([adj[low], adj[high]], axis=0)
        p = jnp.concatenate([r.p0[lead, at], r.p0[tail, at]], axis=0)
        p = jnp.where(allowed_of(b, edges), p, 0.0)
        new = updated(b, edges, p, adj)
        r.p1[lead, at] = new[:WIN]
        r.p1[tail, at] = new[WIN:]
        r.yrow[y, pl.ds(b, 1), :] += fold(new[WIN:])
        moved = (new - p)[WIN:]
        r.accp[0:1, :] += fold(moved * moved)
        inside = pl.ds(slots - WIN, WIN)
        old = jnp.concatenate([p[:WIN], r.p0[head, at], r.p0[inside, at], p[WIN:]], axis=0)
        now = jnp.concatenate([new[:WIN], r.p1[head, at], r.p1[inside, at], new[WIN:]], axis=0)
        w, v = (window(x, dur[pl.ds(b, 1), :], True) for x in (2.0 * now - old, old))
        for first, k in ((0, WIN), (slots - WIN, 3 * WIN)):
            r.wdp[first : first + WIN, at] = 0.5 * (w[k : k + WIN] - v[k : k + WIN])
            keep(w[k : k + WIN], b, first)

    rows_y = spread(r.yrow, y, y_peers, r.s_rowy.at[0, 0], r.s_rowy.at[0, 1])

    def rows_of(side, q):
        return pl.ds(side * half + q * piece, piece)

    def reduced_loads(it, extra, finish):
        paired = set()

        def produce(i):
            owner = lax.rem(z + ORDER[i], RING)
            full = dot(r.ws[...], r.mem[:, pl.ds(pl.multiple_of(owner * pair, pair), pair)])
            full = (full[:slots] + full[slots:]) * (1.0 / WIN)
            r.part[i, 0] = full[:, :share]
            r.part[i, 1] = full[:, share:]
            send(r.part.at[i, 1 - c], r.pairbuf.at[it, i], r.s_pair.at[it, 0, i], r.s_pair.at[it, 1, i], sibling)

        def mine(i, side, q):
            if i not in paired:
                arrived(r.pairbuf.at[it, i], r.s_pair.at[it, 0, i], r.s_pair.at[it, 1, i], sibling)
                paired.add(i)
            at = rows_of(side, q)
            return r.part[i, c, at, :] + r.pairbuf[it, i, at, :]

        def incoming(upward, m, q):
            buf, sems, source = (r.rsu, r.s_up, below) if upward else (r.rsd, r.s_dn, above)
            arrived(buf.at[it, m, q], sems.at[it, 0, m, q], sems.at[it, 1, m, q], source)
            return buf[it, m, q]

        def message(m, q, upward):
            buf, sems, to = (r.rsu, r.s_up, above) if upward else (r.rsd, r.s_dn, below)
            distance = 4 - (m + 1) // 2
            i = ORDER.index(distance if upward else RING - distance)
            side = m % 2 if upward else 1 - m % 2
            value = mine(i, side, q)
            if m >= 2:
                value = value + incoming(upward, m - 2, q)
            at = rows_of(side, q)
            r.part[i, c, at, :] = value
            send(r.part.at[i, c, at, :], buf.at[it, m, q], sems.at[it, 0, m, q], sems.at[it, 1, m, q], to)

        ready = {0: 3, 1: 3, 2: 5, 3: 5, 4: 7, 5: 7}
        done = 0
        for m in range(MESSAGES):
            while done < ready.get(m, RING):
                produce(done)
                done += 1
            for q in range(PIECES):
                message(m, q, True)
                message(m, q, False)
            extra(m)
        i = ORDER.index(0)
        for q in range(PIECES):
            for side in (0, 1):
                value = mine(i, side, q) + incoming(True, 6 - side, q) + incoming(False, 5 + side, q)
                finish(side, q, rows_of(side, q), value)

    def rows_first(m):
        if m == 3:
            rows_y()
            r.xrow[x] = added(r.yrow)
            rows_first.wait = spread(r.xrow, x, x_peers, r.s_rowx.at[0, 0], r.s_rowx.at[0, 1])
        if m == MESSAGES + 1:
            rows_first.wait()
            total = added(r.xrow)
            new, old = total[:blocks], total[blocks:]
            r.tot1[...] = new
            delta = sigma1 * (root - (2.0 * new - old) * (1.0 / root))
            r.a1[...] = assign[...] + delta
            once = jnp.where(mt == 0, 1.0, 0.0)
            r.accp[3:4, :] = once * fold(delta * delta)
            r.accp[4:5, :] = once * fold(delta * (new - old))

    def part_of(hops, side, q=None):
        at = pl.ds(side * half, half) if q is None else rows_of(side, q)
        return (lax.rem(z + hops + RING, RING), c, at, slice(None))

    def pass_on(m, q, upward):
        sems, to = (r.s_up, above) if upward else (r.s_dn, below)
        hops = -(m // 2) if upward else m // 2
        at = part_of(hops, m % 2 if upward else 1 - m % 2, q)
        send(r.ag.at[at], r.ag.at[at], sems.at[0, 2, m, q], sems.at[1, 2, m, q], to)

    def across(hops, side):
        k = 2 * (hops % RING) + side
        at = part_of(hops, side)
        send(r.ag.at[at], r.ag.at[at], r.s_sib.at[0, k], r.s_sib.at[1, k], sibling)

    def finish_first(side, q, at, value):
        old = r.cap_s[at, :]
        new = jnp.maximum(old + sigma1 * (value - r.capac_s[at, :]), 0.0)
        r.ag[z, c, at, :] = new
        pass_on(side, q, True)
        pass_on(1 - side, q, False)
        moved = new - old
        r.accp[1:2, :] += fold(moved * moved)
        if q == PIECES - 1:
            across(0, side)

    reduced_loads(0, rows_first, finish_first)

    def crossed(hops, side):
        k = 2 * (hops % RING) + side
        at = (lax.rem(z + hops + RING, RING), 1 - c, pl.ds(side * half, half), slice(None))
        arrived(r.ag.at[at], r.s_sib.at[0, k], r.s_sib.at[1, k], sibling)

    def gather(hops, first=False):
        crossed(hops, 0)
        crossed(hops, 1)
        owner = lax.rem(z + hops + RING, RING)
        high, low = split(jnp.concatenate([r.ag[owner, 0], r.ag[owner, 1]], axis=1))
        both = jnp.concatenate([high, low], axis=0)
        full = dot(both, r.mem[:, pl.ds(pl.multiple_of(owner * pair, pair), pair)], 1)
        full = full[:slots] + full[slots:]
        r.pj1[own, :] = full if first else r.pj1[own, :] + full

    work = {1: (0,), 3: (-1, 1), 5: (-2, 2), 6: (-3, 3)}
    for m in range(MESSAGES):
        for upward in (True, False):
            hops = -1 - m // 2 if upward else 1 + m // 2
            side = m % 2 if upward else 1 - m % 2
            sems, source = (r.s_up, below) if upward else (r.s_dn, above)
            for q in range(PIECES):
                arrived(r.ag.at[part_of(hops, side, q)], sems.at[0, 2, m, q], sems.at[1, 2, m, q], source)
                if m + 2 < MESSAGES:
                    pass_on(m + 2, q, upward)
            across(hops, side)
        for hops in work.get(m, ()):
            gather(hops, first=hops == 0)
        rows_first(MESSAGES + m)
    gather(4)

    duals_wait = exchange(3, r.pj1)

    @pl.loop(0, blocks, unroll=2)
    def _(b):
        at = lanes_of(b)
        r.accp[2:3, :] += fold((r.pj1[own, at] - r.pj0[own, at]) * r.wdp[:, at]) * (1.0 / WIN)

    r.sc_j[mj] = r.accp[...]
    spread(r.sc_j, mj, j_peers, r.s_scj.at[0], r.s_scj.at[1])()
    r.sc_t[mt] = added(r.sc_j)
    sums_wait = spread(r.sc_t, mt, t_peers, r.s_sct.at[0], r.s_sct.at[1])
    duals_wait()

    @pl.loop(0, blocks, unroll=2)
    def _(b):
        r.grad[:, lanes_of(b)] = cost_of(b) - r.a1[pl.ds(b, 1), :] * (1.0 / root) + adjoint(r.pj1, b)

    sums_wait()
    sums = jnp.sum(added(r.sc_t), axis=1, keepdims=True)
    sum_primal, sum_cap, cross_primal, sum_assign, cross_assign = (sums[k : k + 1] for k in range(5))
    movement = weight * 0.5 * sum_primal + (sum_assign + sum_cap) / (2.0 * weight)
    interaction = jnp.abs(cross_primal - cross_assign * (1.0 / root))
    step_next = movement / (interaction + movement / (1.5 * eta))
    tau2 = jnp.broadcast_to(step_next / weight, (1, LANES))
    sigma2 = jnp.broadcast_to(step_next * weight, (1, LANES))

    drain()

    @pl.loop(0, blocks, unroll=2)
    def _(b):
        at = lanes_of(b)
        p = r.p1[:, at]
        new = jnp.where(allowed_of(b), jnp.maximum(p - tau2 * r.grad[:, at], 0.0), 0.0)
        r.p0[:, at] = new
        r.yrow2[y, pl.ds(b, 1), :] = fold(new[WIN:])
        keep(loaded(2.0 * new - p, b), b)

    rows2_y = spread(r.yrow2, y, y_peers, r.s_rowy.at[1, 0], r.s_rowy.at[1, 1])

    store = pltpu.make_async_copy(r.sd_v, out_p, r.s_out.at[0])

    def rows_second(m):
        if m == 3:
            rows2_y()
            r.xrow2[x] = added(r.yrow2)
            rows_second.wait = spread(r.xrow2, x, x_peers, r.s_rowx.at[1, 0], r.s_rowx.at[1, 1])
        if m == 5:
            rows_second.wait()
            new = added(r.xrow2)
            out_a[...] = r.a1[...] + sigma2 * (root - (2.0 * new - r.tot1[...]) * (1.0 / root))

        if m == 3:

            @pl.loop(0, blocks, unroll=2)
            def _(b):
                r.sd_v[lanes_of(b), :] = r.p0[own, lanes_of(b)].T

            store.start()

    def finish_second(side, q, at, value):
        r.c2[at, :] = jnp.maximum(r.ag[z, c, at, :] + sigma2 * (value - r.capac_s[at, :]), 0.0)

    reduced_loads(1, rows_second, finish_second)
    out_c[...] = r.c2[...].T
    drain()
    store.wait()


def move(p, a, c, p_out, a_out, c_out, p_v, a_v, c_v, sem_in, sem_out):
    rows = p.shape[0] // STRIPS
    ways = [(a, a_v, a_out), (c, c_v, c_out)]
    for k in range(STRIPS):
        at = pl.ds(k * rows, rows)
        ways.append((p.at[at, :], p_v.at[at, :], p_out.at[at, :]))
    copies_in = [pltpu.make_async_copy(w[0], w[1], sem_in.at[k]) for k, w in enumerate(ways)]
    copies_out = [pltpu.make_async_copy(w[1], w[2], sem_out.at[k]) for k, w in enumerate(ways)]
    for copy in copies_in:
        copy.start()
    for before, after in zip(copies_in, copies_out):
        before.wait()
        after.start()
    for copy in copies_out:
        copy.wait()


def shards(sizes, all_slots, start, assign, cap, tool, dur, rel, slack, capac, jw, eta, omega):
    ny, nx = sizes
    rows, slots = start.shape
    tools = cap.shape[0]
    share = tools // (RING * CORES)
    blocks = rows // LANES
    scratch = scratch_of(rows, slots, tools, share, blocks, ny, nx)
    hbm = pl.BlockSpec(memory_space=pltpu.HBM)
    vec = pl.BlockSpec(memory_space=pltpu.VMEM)

    def tiles(v):
        return v.reshape(blocks, LANES)

    results = (
        jax.ShapeDtypeStruct((rows, slots), F32),
        jax.ShapeDtypeStruct((blocks, LANES), F32),
        jax.ShapeDtypeStruct((share, slots), F32),
    )
    found = pl.pallas_call(
        functools.partial(kernel, tuple(scratch), ny, nx, all_slots),
        out_shape=results,
        in_specs=[hbm] * 11,
        out_specs=(hbm, vec, vec),
        scratch_shapes=list(scratch.values()),
        compiler_params=pltpu.CompilerParams(
            collective_id=0, has_side_effects=True, vmem_limit_bytes=58 * 1024 * 1024
        ),
        cost_estimate=pl.CostEstimate(flops=8_600_000_000, bytes_accessed=6_000_000, transcendentals=0),
        name="pdhg",
    )(start, cap, capac, *map(tiles, (tool, dur, rel, slack, jw, assign)), eta, omega)
    p, a, c = pl.pallas_call(
        move,
        out_shape=results,
        in_specs=[hbm] * 3,
        out_specs=(hbm, hbm, hbm),
        scratch_shapes=[pltpu.VMEM(result.shape, F32) for result in results]
        + [pltpu.SemaphoreType.DMA((2 + STRIPS,))] * 2,
        name="move",
    )(*found)
    return p, a.reshape(rows), c


def solution(mesh):
    ntm = mesh.shape["tm"]
    ny = 4 if ntm >= 16 else ntm

    def run(start, *rest):
        body = functools.partial(shards, (ny, ntm // ny), start.shape[1])
        return jax.shard_map(
            body,
            mesh=mesh,
            in_specs=(
                P("jobs", "tm"), P("jobs"), P(None, "tm"), P("jobs"), P("jobs"), P("jobs"),
                P("jobs"), P(None, "tm"), P("jobs"), P(), P(),
            ),
            out_specs=(P("jobs", "tm"), P("jobs"), P("jobs", "tm")),
            check_vma=False,
        )(start, *rest)

    return run
```

```python
import functools
import math
import types

import jax
import jax.numpy as jnp
from jax import lax
from jax.experimental import pallas as pl
from jax.experimental.pallas import tpu as pltpu
from jax.sharding import PartitionSpec as P

WIN = 32
LANES = 128
RING = 8
CORES = 2
F32, BF16 = jnp.float32, jnp.bfloat16
ORDER = (4, 3, 5, 2, 6, 1, 7, 0)
MESSAGES = 7
PIECES = 2
STRIPS = 4


def window(x, dur, backward):
    n = x.shape[0]

    def move(v, k):
        return pltpu.roll(v, k if backward else n - k, 0)

    d = jnp.broadcast_to(dur, x.shape)
    span, total = 1, x
    acc = jnp.where((d & 1) != 0, x, 0.0)
    while span < WIN // 2:
        total = total + move(total, span)
        span *= 2
        acc = jnp.where((d & span) != 0, total + move(acc, span), acc)
    total = total + move(total, span)
    return jnp.where(d == WIN, total, acc)


def summed(x, dur, backward):
    half = (x.shape[0] - WIN) // 2
    parts = (x[: half + WIN], x[half:])
    kept = slice(WIN, None) if backward else slice(0, half)
    return jnp.concatenate([window(part, dur, backward)[kept] for part in parts], axis=0)


def split(x):
    high = x.astype(BF16)
    return high, (x - high.astype(F32)).astype(BF16)


def dot(a, b, contract_b=0):
    return lax.dot_general(
        a, b, (((1,), (contract_b,)), ((), ())), preferred_element_type=F32
    )


def fold(x):
    return jnp.sum(x, axis=0, keepdims=True)


def scratch_of(rows, slots, tools, share, blocks, ny, nx):
    piece = slots // (2 * PIECES)
    dma, vmem = pltpu.SemaphoreType.DMA, pltpu.VMEM
    return dict(
        ints=vmem((4, blocks, LANES), jnp.int32),
        floats=vmem((2, blocks, LANES), F32),
        eta=pltpu.SMEM((1,), F32),
        omega=pltpu.SMEM((1,), F32),
        sd_v=vmem((rows, slots), F32),
        cap_v=vmem((tools, slots), F32),
        capac_v=vmem((share, slots), jnp.int32),
        cap_hi=vmem((tools, slots), BF16),
        cap_lo=vmem((tools, slots), BF16),
        mem=vmem((rows, tools), BF16),
        pj0=vmem((slots + 2 * WIN, rows), F32),
        pj1=vmem((slots + 2 * WIN, rows), F32),
        p0=vmem((slots + WIN, rows), F32),
        p1=vmem((slots + WIN, rows), F32),
        grad=vmem((slots + WIN, rows), F32),
        wdp=vmem((slots, rows), F32),
        ws=vmem((2 * slots, rows), BF16),
        part=vmem((RING, CORES, slots, share), F32),
        pairbuf=vmem((2, RING, slots, share), F32),
        rsu=vmem((2, MESSAGES, PIECES, piece, share), F32),
        rsd=vmem((2, MESSAGES, PIECES, piece, share), F32),
        ag=vmem((RING, CORES, slots, share), F32),
        cap_s=vmem((slots, share), F32),
        capac_s=vmem((slots, share), F32),
        c2=vmem((slots, share), F32),
        yrow=vmem((ny, 2 * blocks, LANES), F32),
        xrow=vmem((nx, 2 * blocks, LANES), F32),
        yrow2=vmem((ny, blocks, LANES), F32),
        xrow2=vmem((nx, blocks, LANES), F32),
        tot1=vmem((blocks, LANES), F32),
        a1=vmem((blocks, LANES), F32),
        accp=vmem((8, LANES), F32),
        sc_j=vmem((RING * CORES, 8, LANES), F32),
        sc_t=vmem((ny * nx, 8, LANES), F32),
        s_load=dma((11,)),
        s_out=dma((1,)),
        s_halo=dma((2, 5)),
        s_up=dma((2, 3, MESSAGES, PIECES)),
        s_dn=dma((2, 3, MESSAGES, PIECES)),
        s_pair=dma((2, 2, RING)),
        s_sib=dma((2, 2 * RING)),
        s_rowy=dma((2, 2, ny)),
        s_rowx=dma((2, 2, nx)),
        s_scj=dma((2, RING * CORES)),
        s_sct=dma((2, ny * nx)),
    )


def kernel(
    names, ny, nx, all_slots, sd, cap, capac, tool_in, dur_in, rel_in, slack_in, jw_in, assign_in,
    eta_in, omega_in, out_p, out_a, out_c, *scratch,
):
    r = types.SimpleNamespace(**dict(zip(names, scratch)))
    rows, slots = r.sd_v.shape
    tools, share = r.cap_v.shape[0], r.capac_v.shape[0]
    blocks, half, ntm = rows // LANES, slots // 2, ny * nx
    piece = half // PIECES
    pair = CORES * share
    root = math.sqrt(all_slots)

    mj, mt = lax.axis_index("jobs"), lax.axis_index("tm")
    z, c = lax.div(mj, CORES), lax.rem(mj, CORES)
    x, y = lax.div(mt, ny), lax.rem(mt, ny)

    def zline(k):
        return lax.rem(z + k, RING) * CORES + c

    sibling = (z * CORES + 1 - c, mt)
    above, below = (zline(1), mt), (zline(RING - 1), mt)
    after, before = (mj, lax.rem(mt + 1, ntm)), (mj, lax.rem(mt + ntm - 1, ntm))
    far = sorted(range(1, RING * CORES), key=lambda k: -min(k, RING * CORES - k))
    j_peers = [(lax.rem(mj + k, RING * CORES), (lax.rem(mj + k, RING * CORES), mt)) for k in far]
    y_peers = [(lax.rem(y + k, ny), (mj, x * ny + lax.rem(y + k, ny))) for k in range(1, ny)]
    x_peers = [(lax.rem(x + k, nx), (mj, lax.rem(x + k, nx) * ny + y)) for k in range(1, nx)]

    moves = [(i, j) for i in range(nx) for j in range(ny) if i or j]
    moves.sort(key=lambda v: -min(v[0], nx - v[0]) - min(v[1], ny - v[1]))
    t_peers = [lax.rem(x + i, nx) * ny + lax.rem(y + j, ny) for i, j in moves]
    t_peers = [(k, (mj, k)) for k in t_peers]
    tool, dur, rel, slack = (r.ints.at[k] for k in range(4))
    jw, assign = (r.floats.at[k] for k in range(2))

    sent = []

    def remote(src, dst, ssem, rsem, device):
        return pltpu.make_async_remote_copy(
            src_ref=src, dst_ref=dst, send_sem=ssem, recv_sem=rsem,
            device_id=device, device_id_type=pl.DeviceIdType.MESH,
        )

    def send(*args):
        copy = remote(*args)
        copy.start()
        sent.append(copy)

    def arrived(dst, ssem, rsem, device):
        remote(dst, dst, ssem, rsem, device).wait_recv()

    def drain():
        for copy in sent:
            copy.wait_send()
        sent.clear()

    def spread(buf, mine, peers, ssem, rsem):
        for k, (_, device) in enumerate(peers):
            send(buf.at[mine], buf.at[mine], ssem.at[k], rsem.at[mine], device)

        def wait():
            for k, (index, device) in enumerate(peers):
                arrived(buf.at[index], ssem.at[k], rsem.at[index], device)

        return wait

    def added(buf):
        total = buf[0]
        for k in range(1, buf.shape[0]):
            total = total + buf[k]
        return total

    barrier = pltpu.get_barrier_semaphore()
    partners = [sibling, above, below, before, after]
    partners += [device for group in (y_peers, x_peers) for _, device in group]
    for device in partners:
        pl.semaphore_signal(barrier, inc=1, device_id=device, device_id_type=pl.DeviceIdType.MESH)
    first_tool = pl.multiple_of(mj * share, share)
    loads = [
        pltpu.make_async_copy(source, target, r.s_load.at[k])
        for k, (source, target) in enumerate(
            [
                (tool_in, tool), (cap, r.cap_v), (sd, r.sd_v), (dur_in, dur), (rel_in, rel), (slack_in, slack),
                (jw_in, jw), (assign_in, assign), (eta_in, r.eta), (omega_in, r.omega),
                (capac.at[pl.ds(first_tool, share), :], r.capac_v),
            ]
        )
    ]
    for copy in loads:
        copy.start()
    loads[0].wait()

    lane = lax.broadcasted_iota(jnp.int32, (LANES, LANES), 1).astype(F32)

    @pl.loop(0, blocks, unroll=2)
    def _(b):
        row = jnp.broadcast_to(tool[pl.ds(b, 1), :].astype(F32), (LANES, LANES))
        column = row.T
        for k in range(tools // LANES):
            hit = jnp.where(column == lane + float(k * LANES), 1.0, 0.0).astype(BF16)
            r.mem[pl.ds(pl.multiple_of(b * LANES, LANES), LANES), k * LANES : (k + 1) * LANES] = hit

    loads[1].wait()

    @pl.loop(0, tools // share)
    def _(b):
        at = pl.ds(pl.multiple_of(b * share, share), share)
        high, low = split(r.cap_v[at, :])
        r.cap_hi[at, :] = high
        r.cap_lo[at, :] = low

    step = min(rows, 256)

    @pl.loop(0, rows // step)
    def _(b):
        at = pl.ds(pl.multiple_of(b * step, step), step)
        m = r.mem[at, :]
        found = dot(m, r.cap_hi[...]) + dot(m, r.cap_lo[...])
        r.pj0[WIN : WIN + slots, at] = found.T

    def lanes_of(b):
        return pl.ds(pl.multiple_of(b * LANES, LANES), LANES)

    slot = lax.broadcasted_iota(jnp.int32, (slots + WIN, LANES), 0) + (mt * slots - WIN)
    own = slice(WIN, WIN + slots)

    def allowed_of(b, s=slot):
        return (s >= rel[pl.ds(b, 1), :]) & (s + dur[pl.ds(b, 1), :] <= all_slots)

    def cost_of(b, s=slot):
        d = dur[pl.ds(b, 1), :]
        due = rel[pl.ds(b, 1), :] + d + slack[pl.ds(b, 1), :]
        end = s + d
        late = jnp.maximum(end - due, 0)
        return jw[pl.ds(b, 1), :] * (
            end.astype(F32) * (1.0 / all_slots) + late.astype(F32) * (1.0 / (4 * WIN))
        )

    for copy in loads[2:]:
        copy.wait()
    weight, eta = r.omega[0], r.eta[0]
    tau1, sigma1 = eta / weight, eta * weight

    @pl.loop(0, blocks, unroll=2)
    def _(b):
        start = r.sd_v[lanes_of(b), :].T
        p = jnp.where(allowed_of(b, slot[WIN:]), start, 0.0)
        r.p0[own, lanes_of(b)] = p
        r.yrow[y, pl.ds(blocks + b, 1), :] = fold(p)

    pl.semaphore_wait(barrier, len(partners))

    def halo(k, src, dst, device):
        send(src, dst, r.s_halo.at[0, k], r.s_halo.at[1, k], device)

    def halo_arrived(k, dst, device):
        arrived(dst, r.s_halo.at[0, k], r.s_halo.at[1, k], device)

    lead, head = pl.ds(0, WIN), pl.ds(WIN, WIN)
    tail, beyond = pl.ds(slots, WIN), pl.ds(slots + WIN, WIN)

    def exchange(k, buf):
        halo(k, buf.at[head, :], buf.at[beyond, :], before)
        halo(k + 1, buf.at[tail, :], buf.at[lead, :], after)

        def wait():
            halo_arrived(k, buf.at[beyond, :], after)
            halo_arrived(k + 1, buf.at[lead, :], before)

        return wait

    duals_wait = exchange(0, r.pj0)
    halo(2, r.p0.at[tail, :], r.p0.at[lead, :], after)

    r.cap_s[...] = r.cap_v[pl.ds(first_tool, share), :].T
    r.capac_s[...] = r.capac_v[...].astype(F32).T

    def adjoint(buf, b):
        at = lanes_of(b)
        past = jnp.where(mt == ntm - 1, 0.0, buf[beyond, at])
        x = jnp.concatenate([buf[0 : slots + WIN, at], past], axis=0)
        return summed(x, dur[pl.ds(b, 1), :], False) * (1.0 / WIN)

    def loaded(x, b):
        return summed(x, dur[pl.ds(b, 1), :], True)

    def keep(w, b, first=0):
        high, low = split(w)
        n = w.shape[0]
        r.ws[first : first + n, lanes_of(b)] = high
        r.ws[slots + first : slots + first + n, lanes_of(b)] = low

    inner = slice(WIN, slots)
    r.accp[...] = jnp.zeros_like(r.accp)

    def updated(b, s, p, adj):
        gradient = cost_of(b, s) - assign[pl.ds(b, 1), :] * (1.0 / root) + adj * (1.0 / WIN)
        return jnp.where(allowed_of(b, s), jnp.maximum(p - tau1 * gradient, 0.0), 0.0)

    @pl.loop(0, blocks, unroll=2)
    def _(b):
        at = lanes_of(b)
        p = r.p0[inner, at]
        adj = summed(r.pj0[own, at], dur[pl.ds(b, 1), :], False)
        new = updated(b, slot[inner], p, adj)
        r.p1[inner, at] = new
        r.yrow[y, pl.ds(b, 1), :] = fold(new)
        moved = new - p
        r.accp[0:1, :] += fold(moved * moved)
        w = loaded(2.0 * new - p, b)
        r.wdp[WIN : slots - WIN, at] = 0.5 * (w - loaded(p, b))
        keep(w, b, WIN)

    duals_wait()
    halo_arrived(2, r.p0.at[lead, :], before)
    low, high = slice(0, WIN), slice(2 * WIN, 3 * WIN)
    edges = jnp.concatenate([slot[:WIN], slot[slots:]], axis=0)

    @pl.loop(0, blocks, unroll=2)
    def _(b):
        at = lanes_of(b)
        past = jnp.where(mt == ntm - 1, 0.0, r.pj0[beyond, at])
        bands = jnp.concatenate([r.pj0[: 2 * WIN, at], r.pj0[tail, at], past], axis=0)
        adj = window(bands, dur[pl.ds(b, 1), :], False)
        adj = jnp.concatenate([adj[low], adj[high]], axis=0)
        p = jnp.concatenate([r.p0[lead, at], r.p0[tail, at]], axis=0)
        p = jnp.where(allowed_of(b, edges), p, 0.0)
        new = updated(b, edges, p, adj)
        r.p1[lead, at] = new[:WIN]
        r.p1[tail, at] = new[WIN:]
        r.yrow[y, pl.ds(b, 1), :] += fold(new[WIN:])
        moved = (new - p)[WIN:]
        r.accp[0:1, :] += fold(moved * moved)
        inside = pl.ds(slots - WIN, WIN)
        old = jnp.concatenate([p[:WIN], r.p0[head, at], r.p0[inside, at], p[WIN:]], axis=0)
        now = jnp.concatenate([new[:WIN], r.p1[head, at], r.p1[inside, at], new[WIN:]], axis=0)
        w, v = (window(x, dur[pl.ds(b, 1), :], True) for x in (2.0 * now - old, old))
        for first, k in ((0, WIN), (slots - WIN, 3 * WIN)):
            r.wdp[first : first + WIN, at] = 0.5 * (w[k : k + WIN] - v[k : k + WIN])
            keep(w[k : k + WIN], b, first)

    rows_y = spread(r.yrow, y, y_peers, r.s_rowy.at[0, 0], r.s_rowy.at[0, 1])

    def rows_of(side, q):
        return pl.ds(side * half + q * piece, piece)

    def reduced_loads(it, extra, finish):
        paired = set()

        def produce(i):
            owner = lax.rem(z + ORDER[i], RING)
            full = dot(r.ws[...], r.mem[:, pl.ds(pl.multiple_of(owner * pair, pair), pair)])
            full = (full[:slots] + full[slots:]) * (1.0 / WIN)
            r.part[i, 0] = full[:, :share]
            r.part[i, 1] = full[:, share:]
            send(r.part.at[i, 1 - c], r.pairbuf.at[it, i], r.s_pair.at[it, 0, i], r.s_pair.at[it, 1, i], sibling)

        def mine(i, side, q):
            if i not in paired:
                arrived(r.pairbuf.at[it, i], r.s_pair.at[it, 0, i], r.s_pair.at[it, 1, i], sibling)
                paired.add(i)
            at = rows_of(side, q)
            return r.part[i, c, at, :] + r.pairbuf[it, i, at, :]

        def incoming(upward, m, q):
            buf, sems, source = (r.rsu, r.s_up, below) if upward else (r.rsd, r.s_dn, above)
            arrived(buf.at[it, m, q], sems.at[it, 0, m, q], sems.at[it, 1, m, q], source)
            return buf[it, m, q]

        def message(m, q, upward):
            buf, sems, to = (r.rsu, r.s_up, above) if upward else (r.rsd, r.s_dn, below)
            distance = 4 - (m + 1) // 2
            i = ORDER.index(distance if upward else RING - distance)
            side = m % 2 if upward else 1 - m % 2
            value = mine(i, side, q)
            if m >= 2:
                value = value + incoming(upward, m - 2, q)
            at = rows_of(side, q)
            r.part[i, c, at, :] = value
            send(r.part.at[i, c, at, :], buf.at[it, m, q], sems.at[it, 0, m, q], sems.at[it, 1, m, q], to)

        ready = {0: 2, 1: 3, 2: 5, 3: 5, 4: 7, 5: 7}
        done = 0
        for m in range(MESSAGES):
            while done < ready.get(m, RING):
                produce(done)
                done += 1
            for q in range(PIECES):
                message(m, q, True)
                message(m, q, False)
            extra(m)
        i = ORDER.index(0)
        for q in range(PIECES):
            for side in (0, 1):
                value = mine(i, side, q) + incoming(True, 6 - side, q) + incoming(False, 5 + side, q)
                finish(side, q, rows_of(side, q), value)

    def rows_first(m):
        if m == 3:
            rows_y()
            r.xrow[x] = added(r.yrow)
            rows_first.wait = spread(r.xrow, x, x_peers, r.s_rowx.at[0, 0], r.s_rowx.at[0, 1])
        if m == MESSAGES + 1:
            rows_first.wait()
            total = added(r.xrow)
            new, old = total[:blocks], total[blocks:]
            r.tot1[...] = new
            delta = sigma1 * (root - (2.0 * new - old) * (1.0 / root))
            r.a1[...] = assign[...] + delta
            once = jnp.where(mt == 0, 1.0, 0.0)
            r.accp[3:4, :] = once * fold(delta * delta)
            r.accp[4:5, :] = once * fold(delta * (new - old))

    def part_of(hops, side, q=None):
        at = pl.ds(side * half, half) if q is None else rows_of(side, q)
        return (lax.rem(z + hops + RING, RING), c, at, slice(None))

    def pass_on(m, q, upward):
        sems, to = (r.s_up, above) if upward else (r.s_dn, below)
        hops = -(m // 2) if upward else m // 2
        at = part_of(hops, m % 2 if upward else 1 - m % 2, q)
        send(r.ag.at[at], r.ag.at[at], sems.at[0, 2, m, q], sems.at[1, 2, m, q], to)

    def across(hops, side):
        k = 2 * (hops % RING) + side
        at = part_of(hops, side)
        send(r.ag.at[at], r.ag.at[at], r.s_sib.at[0, k], r.s_sib.at[1, k], sibling)

    def finish_first(side, q, at, value):
        old = r.cap_s[at, :]
        new = jnp.maximum(old + sigma1 * (value - r.capac_s[at, :]), 0.0)
        r.ag[z, c, at, :] = new
        pass_on(side, q, True)
        pass_on(1 - side, q, False)
        moved = new - old
        r.accp[1:2, :] += fold(moved * moved)
        if q == PIECES - 1:
            across(0, side)

    reduced_loads(0, rows_first, finish_first)

    def crossed(hops, side):
        k = 2 * (hops % RING) + side
        at = (lax.rem(z + hops + RING, RING), 1 - c, pl.ds(side * half, half), slice(None))
        arrived(r.ag.at[at], r.s_sib.at[0, k], r.s_sib.at[1, k], sibling)

    def gather(hops, first=False):
        crossed(hops, 0)
        crossed(hops, 1)
        owner = lax.rem(z + hops + RING, RING)
        high, low = split(jnp.concatenate([r.ag[owner, 0], r.ag[owner, 1]], axis=1))
        both = jnp.concatenate([high, low], axis=0)
        full = dot(both, r.mem[:, pl.ds(pl.multiple_of(owner * pair, pair), pair)], 1)
        full = full[:slots] + full[slots:]
        r.pj1[own, :] = full if first else r.pj1[own, :] + full

    work = {1: (0,), 3: (-1, 1), 5: (-2, 2), 6: (-3, 3)}
    for m in range(MESSAGES):
        for upward in (True, False):
            hops = -1 - m // 2 if upward else 1 + m // 2
            side = m % 2 if upward else 1 - m % 2
            sems, source = (r.s_up, below) if upward else (r.s_dn, above)
            for q in range(PIECES):
                arrived(r.ag.at[part_of(hops, side, q)], sems.at[0, 2, m, q], sems.at[1, 2, m, q], source)
                if m + 2 < MESSAGES:
                    pass_on(m + 2, q, upward)
            across(hops, side)
        for hops in work.get(m, ()):
            gather(hops, first=hops == 0)
        rows_first(MESSAGES + m)
    gather(4)

    duals_wait = exchange(3, r.pj1)

    @pl.loop(0, blocks, unroll=2)
    def _(b):
        at = lanes_of(b)
        r.accp[2:3, :] += fold((r.pj1[own, at] - r.pj0[own, at]) * r.wdp[:, at]) * (1.0 / WIN)

    r.sc_j[mj] = r.accp[...]
    spread(r.sc_j, mj, j_peers, r.s_scj.at[0], r.s_scj.at[1])()
    r.sc_t[mt] = added(r.sc_j)
    sums_wait = spread(r.sc_t, mt, t_peers, r.s_sct.at[0], r.s_sct.at[1])
    duals_wait()

    @pl.loop(0, blocks, unroll=2)
    def _(b):
        r.grad[:, lanes_of(b)] = cost_of(b) - r.a1[pl.ds(b, 1), :] * (1.0 / root) + adjoint(r.pj1, b)

    sums_wait()
    sums = jnp.sum(added(r.sc_t), axis=1, keepdims=True)
    sum_primal, sum_cap, cross_primal, sum_assign, cross_assign = (sums[k : k + 1] for k in range(5))
    movement = weight * 0.5 * sum_primal + (sum_assign + sum_cap) / (2.0 * weight)
    interaction = jnp.abs(cross_primal - cross_assign * (1.0 / root))
    step_next = movement / (interaction + movement / (1.5 * eta))
    tau2 = jnp.broadcast_to(step_next / weight, (1, LANES))
    sigma2 = jnp.broadcast_to(step_next * weight, (1, LANES))

    drain()

    @pl.loop(0, blocks, unroll=2)
    def _(b):
        at = lanes_of(b)
        p = r.p1[:, at]
        new = jnp.where(allowed_of(b), jnp.maximum(p - tau2 * r.grad[:, at], 0.0), 0.0)
        r.p0[:, at] = new
        r.yrow2[y, pl.ds(b, 1), :] = fold(new[WIN:])
        keep(loaded(2.0 * new - p, b), b)

    rows2_y = spread(r.yrow2, y, y_peers, r.s_rowy.at[1, 0], r.s_rowy.at[1, 1])

    store = pltpu.make_async_copy(r.sd_v, out_p, r.s_out.at[0])

    def rows_second(m):
        if m == 3:
            rows2_y()
            r.xrow2[x] = added(r.yrow2)
            rows_second.wait = spread(r.xrow2, x, x_peers, r.s_rowx.at[1, 0], r.s_rowx.at[1, 1])
        if m == 5:
            rows_second.wait()
            new = added(r.xrow2)
            out_a[...] = r.a1[...] + sigma2 * (root - (2.0 * new - r.tot1[...]) * (1.0 / root))

        if m == 3:

            @pl.loop(0, blocks, unroll=2)
            def _(b):
                r.sd_v[lanes_of(b), :] = r.p0[own, lanes_of(b)].T

            store.start()

    def finish_second(side, q, at, value):
        r.c2[at, :] = jnp.maximum(r.ag[z, c, at, :] + sigma2 * (value - r.capac_s[at, :]), 0.0)

    reduced_loads(1, rows_second, finish_second)
    out_c[...] = r.c2[...].T
    drain()
    store.wait()


def move(p, a, c, p_out, a_out, c_out, p_v, a_v, c_v, sem_in, sem_out):
    rows = p.shape[0] // STRIPS
    ways = [(a, a_v, a_out), (c, c_v, c_out)]
    for k in range(STRIPS):
        at = pl.ds(k * rows, rows)
        ways.append((p.at[at, :], p_v.at[at, :], p_out.at[at, :]))
    copies_in = [pltpu.make_async_copy(w[0], w[1], sem_in.at[k]) for k, w in enumerate(ways)]
    copies_out = [pltpu.make_async_copy(w[1], w[2], sem_out.at[k]) for k, w in enumerate(ways)]
    for copy in copies_in:
        copy.start()
    for before, after in zip(copies_in, copies_out):
        before.wait()
        after.start()
    for copy in copies_out:
        copy.wait()


def shards(sizes, all_slots, start, assign, cap, tool, dur, rel, slack, capac, jw, eta, omega):
    ny, nx = sizes
    rows, slots = start.shape
    tools = cap.shape[0]
    share = tools // (RING * CORES)
    blocks = rows // LANES
    scratch = scratch_of(rows, slots, tools, share, blocks, ny, nx)
    hbm = pl.BlockSpec(memory_space=pltpu.HBM)
    vec = pl.BlockSpec(memory_space=pltpu.VMEM)

    def tiles(v):
        return v.reshape(blocks, LANES)

    results = (
        jax.ShapeDtypeStruct((rows, slots), F32),
        jax.ShapeDtypeStruct((blocks, LANES), F32),
        jax.ShapeDtypeStruct((share, slots), F32),
    )
    found = pl.pallas_call(
        functools.partial(kernel, tuple(scratch), ny, nx, all_slots),
        out_shape=results,
        in_specs=[hbm] * 11,
        out_specs=(hbm, vec, vec),
        scratch_shapes=list(scratch.values()),
        compiler_params=pltpu.CompilerParams(
            collective_id=0, has_side_effects=True, vmem_limit_bytes=58 * 1024 * 1024
        ),
        cost_estimate=pl.CostEstimate(flops=8_600_000_000, bytes_accessed=6_000_000, transcendentals=0),
        name="pdhg",
    )(start, cap, capac, *map(tiles, (tool, dur, rel, slack, jw, assign)), eta, omega)
    p, a, c = pl.pallas_call(
        move,
        out_shape=results,
        in_specs=[hbm] * 3,
        out_specs=(hbm, hbm, hbm),
        scratch_shapes=[pltpu.VMEM(result.shape, F32) for result in results]
        + [pltpu.SemaphoreType.DMA((2 + STRIPS,))] * 2,
        name="move",
    )(*found)
    return p, a.reshape(rows), c


def solution(mesh):
    ntm = mesh.shape["tm"]
    ny = 4 if ntm >= 16 else ntm

    def run(start, *rest):
        body = functools.partial(shards, (ny, ntm // ny), start.shape[1])
        return jax.shard_map(
            body,
            mesh=mesh,
            in_specs=(
                P("jobs", "tm"), P("jobs"), P(None, "tm"), P("jobs"), P("jobs"), P("jobs"),
                P("jobs"), P(None, "tm"), P("jobs"), P(), P(),
            ),
            out_specs=(P("jobs", "tm"), P("jobs"), P("jobs", "tm")),
            check_vma=False,
        )(start, *rest)

    return run
```
